128 devices in a mesh: dom: 32 (over x, z_lo, y), sub: 4 (over z_hi, core).
Axes of the slice: x: 4, y: 4, z: 4 (z_hi: 2, z_lo: 2; z = z_hi * 2 + z_lo), core: 2. Of those that a mesh axis runs over, the one named last changes fastest.
Arguments:
- features: bfloat16 [65536, 128], P(('dom', 'sub')), may hold values from -6 to 6
- frac: float32 [3, 65536], P(None, ('dom', 'sub')), may hold values from 0 to 1
- k_int: int32 [3, 1024], replicated, may hold values from -6 to 6
- kernel: float32 [1024], replicated, may hold values from 0.05 to 1
- dist: float32 [65536, 64], P(('dom', 'sub')), may hold values from 0.8 to 7
- nbr: int32 [65536, 64], P(('dom', 'sub')), may hold values from 0 to 767, as said below
- send_index: int32 [128, 2, 128], P(('dom', 'sub')), may hold values from 0 to 511, as said below
- counts: int32 [128], P(('dom', 'sub')), may hold values from 256 to 512, as said below
- cot: bfloat16 [65536, 128], P(('dom', 'sub')), may hold values from -6 to 6
- w_msg: bfloat16 [128, 128], replicated, may hold values from -0.5 to 0.5
- w_rad: bfloat16 [16, 128], replicated, may hold values from -1.5 to 1.5
- w_q: bfloat16 [128, 128], replicated, may hold values from -0.5 to 0.5
- w_o: bfloat16 [128, 128], replicated, may hold values from -0.5 to 0.5
Outputs:
- grad_features: float32 [65536, 128], P(('dom', 'sub'))
- grad_w_msg: float32 [128, 128], replicated
- grad_w_rad: float32 [16, 128], replicated
- grad_w_q: float32 [128, 128], replicated
- grad_w_o: float32 [128, 128], replicated
The draws below stay inside these ranges and needn't reach their ends.
Inputs may be any that keep to these rules, and one draw needn't show every extreme that they name: One device has counts = 512. `nbr`: a slot value below 512 names a local row below the device's count (a live atom); a slot r >= 512 names ghost row r - 512 of ext; the slots of local rows b * 128 to (b + 1) * 128 - 1 name ghost rows or local rows w to w + 255, with w = min(max(b * 128 - 128 // 2, 0), 256). `send_index`: every entry is below the device's count; entries may repeat.
All inputs are finite; a program needn't handle non-finite values.
Results may differ from the reference program's by a relative error of at most 0.0061.
Values may be sent and summed in bfloat16 or wider, within the bound.
A program may use at most 64 MiB of HBM per device.

```python
import math
import jax
import jax.numpy as jnp
from jax import lax

C = 128
K = 1024
NB = 16
NBR = 64
ATOM_DEV = 512
GHOST = 128
ATOMS = 65536
DEVICES = 128


def atom_counts(key):
    key = jax.random.fold_in(key, 11)
    first, second = jax.random.split(key)
    shortfall = jax.random.randint(first, (DEVICES,), 0, ATOM_DEV // 2 + 1)
    fullest = jax.random.randint(second, (), 0, DEVICES)
    shortfall = jnp.where(jnp.arange(DEVICES) == fullest, 0, shortfall)
    return (ATOM_DEV - shortfall).astype(jnp.int32)


def draw_counts(key, part):
    return atom_counts(key)


def draw_nbr(key, part):
    filled = atom_counts(key)
    key = jax.random.fold_in(key, 3)
    block = min(128, ATOM_DEV)
    window = min(2 * block, ATOM_DEV)
    rows_all = jnp.arange(ATOMS, dtype=jnp.int32)
    local = rows_all % ATOM_DEV
    owner = rows_all // ATOM_DEV
    wstart = jnp.clip(local // block * block - block // 2, 0, ATOM_DEV - window)
    live_in = jnp.clip(filled[owner] - wstart, 0, window)
    span = live_in + 2 * GHOST
    picked = jax.random.randint(key, (ATOMS, NBR), 0, span[:, None])
    slot_ids = jnp.arange(NBR)[None, :]
    first_row = (local == 0)[:, None]
    picked = jnp.where(first_row & (slot_ids == 0), span[:, None] - 1, picked)
    picked = jnp.where(first_row & (slot_ids == 1), 0, picked)
    return jnp.where(picked < live_in[:, None], wstart[:, None] + picked, ATOM_DEV + picked - live_in[:, None]).astype(jnp.int32)


def draw_send_index(key, part):
    filled = atom_counts(key)
    key = jax.random.fold_in(key, 5)
    picked = jax.random.randint(key, (DEVICES, 2, GHOST), 0, filled[:, None, None])
    corner = (jnp.arange(2) == 0)[:, None] & (jnp.arange(GHOST) == 0)[None, :]
    picked = jnp.where(corner[None], filled[:, None, None] - 1, picked)
    return picked.astype(jnp.int32)


def touch_ends(array, rng, least, high):
    index_at = [jax.random.randint(jax.random.fold_in(rng, axis), (), 0, length) for axis, length in enumerate(array.shape)]
    widest = array.shape.index(max(array.shape))
    neighbour = index_at[:widest] + [(index_at[widest] + 1) % array.shape[widest]] + index_at[widest + 1:]
    return array.at[tuple(index_at)].set(least).at[tuple(neighbour)].set(high)


def level_of(own_key, shape, cuts, low, top_value):
    factor_of = 1.0
    for axis_at, parts in cuts:
        draws = jax.random.uniform(jax.random.fold_in(jax.random.fold_in(own_key, 6), axis_at), (parts,), jnp.float32, low / len(cuts), top_value / len(cuts))
        factor_of = factor_of * jnp.repeat(jnp.exp(draws), shape[axis_at] // parts).reshape((-1,) + (1,) * (len(shape) - 1 - axis_at))
    return factor_of


def centred(key, shape, scale, most, cuts=(), kind=jnp.bfloat16):
    gain = level_of(key, shape, cuts, -0.22, 0.18) if cuts else 1.0
    array = jax.random.normal(key, shape, jnp.float32) * scale * gain
    return jnp.minimum(jnp.maximum(array, -most), most).astype(kind)


def setup_inputs(seed: int = 0) -> dict:
    streams_of = jax.random.split(jax.random.key(seed), 14)
    return {
        "features": centred(streams_of[0], (ATOMS, C), 1.0, 6.0, ((0, 128),)),
        "frac": jnp.clip(1.0 * jax.random.uniform(streams_of[1], (3, ATOMS), jnp.float32) ** level_of(streams_of[1], (3, ATOMS), ((1, 128),), -0.2, 0.2), 0.0, 1.0),
        "k_int": touch_ends(jax.random.randint(streams_of[2], (3, K), -6, 7), jax.random.fold_in(streams_of[2], 1), -6, 6).astype(jnp.int32),
        "kernel": jnp.clip(jnp.exp(jax.random.uniform(streams_of[3], (K,), jnp.float32, math.log(0.05), math.log(1.0))), 0.05, 1.0),
        "dist": jnp.clip(0.8 + 6.2 * jax.random.uniform(streams_of[4], (ATOMS, NBR), jnp.float32) ** level_of(streams_of[4], (ATOMS, NBR), ((0, 128),), -0.2, 0.2), 0.8, 7.0),
        "nbr": draw_nbr(jax.random.fold_in(streams_of[13], 71), 0),
        "send_index": draw_send_index(jax.random.fold_in(streams_of[13], 71), 0),
        "counts": draw_counts(jax.random.fold_in(streams_of[13], 71), 0),
        "cot": centred(streams_of[8], (ATOMS, C), 1.0, 6.0, ((0, 128),)),
        "w_msg": centred(streams_of[9], (C, C), C ** -0.5, 0.5),
        "w_rad": centred(streams_of[10], (NB, C), NB ** -0.5, 1.5),
        "w_q": centred(streams_of[11], (C, C), C ** -0.5, 0.5),
        "w_o": centred(streams_of[12], (C, C), C ** -0.5, 0.5),
    }


cutoff = 6.0
spread = 0.4
two_pi = 2.0 * math.pi

def radial_basis(flat_dist, count_b):
    centers = (cutoff * jnp.arange(count_b, dtype=jnp.float32) / (count_b - 1))[:, None]
    envelope = jnp.square(jnp.maximum(0.0, 1.0 - flat_dist / cutoff))
    return jnp.exp(-jnp.square((flat_dist[None, :] - centers) / spread)) * envelope[None, :]

def edge_terms(u_ext, dist, nbr, g_out, w_rad, rows):
    atoms, slots = dist.shape
    chans = u_ext.shape[1]
    basis = radial_basis(dist.reshape(-1), w_rad.shape[0])
    filt = lax.dot_general(basis, w_rad.astype(jnp.float32), (((0,), (0,)), ((), ())), precision=lax.Precision.HIGHEST)
    flat = nbr.reshape(-1)
    ugot = u_ext[flat].astype(jnp.float32)
    pre = lax.optimization_barrier(jnp.sum((ugot * filt).reshape(atoms, slots, chans), axis=1))
    sig = jax.nn.sigmoid(pre)
    gpre = g_out * sig * (1.0 + pre * (1.0 - sig))
    gfilt = (gpre[:, None, :] * ugot.reshape(atoms, slots, chans)).reshape(-1, chans)
    rad = lax.dot_general(basis, gfilt, (((1,), (0,)), ((), ())), precision=lax.Precision.HIGHEST)
    gedge = (gpre[:, None, :] * filt.reshape(atoms, slots, chans)).reshape(-1, chans)
    gu = jax.ops.segment_sum(gedge, flat, num_segments=rows)
    return (gu, rad)

def phase_tables(k_real, piece):
    turns = k_real[0][:, None] * piece[0][None, :] + k_real[1][:, None] * piece[1][None, :] + k_real[2][:, None] * piece[2][None, :]
    turns = turns - jnp.floor(turns)
    angle = two_pi * turns
    return (jnp.cos(angle).astype(jnp.bfloat16), jnp.sin(angle).astype(jnp.bfloat16))

def reference(features, frac, k_int, kernel, dist, nbr, send_index, counts, cot, w_msg, w_rad, w_q, w_o):
    devices = DEVICES
    width = ATOM_DEV
    ghosts = GHOST
    chans = features.shape[1]
    hfeat = features.reshape(devices, width, chans)
    live = (jnp.arange(width, dtype=jnp.int32)[None, :] < counts[:, None])[..., None]
    g_out = jnp.where(live, cot.reshape(devices, width, chans).astype(jnp.float32), jnp.float32(0.0))
    g_bf = g_out.astype(jnp.bfloat16)
    picks = send_index.reshape(devices, 2 * ghosts)
    outgoing = jax.vmap(lambda rows_in, where_to: rows_in[where_to])(hfeat, picks)
    ext = jnp.concatenate([hfeat, jnp.roll(outgoing[:, ghosts:], 1, axis=0), jnp.roll(outgoing[:, :ghosts], -1, axis=0)], axis=1)

    def short_range(item):
        ext_d, dist_d, nbr_d, go_d = item
        u_ext = jnp.dot(ext_d, w_msg, preferred_element_type=jnp.float32).astype(jnp.bfloat16)
        return edge_terms(u_ext, dist_d, nbr_d, go_d, w_rad, width + 2 * ghosts)
    gu, rad = lax.map(short_range, (ext, dist.reshape(devices, width, NBR), nbr.reshape(devices, width, NBR), g_out))
    gu_b = gu.astype(jnp.bfloat16)
    gh = jnp.einsum('dae,ce->dac', gu_b.astype(jnp.float32), w_msg.astype(jnp.float32), precision=lax.Precision.HIGHEST)
    back_low = jnp.roll(gh[:, width + ghosts:], 1, axis=0)
    back_high = jnp.roll(gh[:, width:width + ghosts], -1, axis=0)
    returned = jnp.concatenate([back_low, back_high], axis=1)
    scattered = jax.vmap(lambda base, where_to, vals: base.at[where_to].add(vals))(jnp.zeros((devices, width, chans), jnp.float32), picks, returned)
    grad_h = g_out + gh[:, :width] + scattered
    q_b = jnp.where(live, jnp.einsum('dac,ce->dae', hfeat.astype(jnp.float32), w_q.astype(jnp.float32), precision=lax.Precision.HIGHEST), jnp.float32(0.0)).astype(jnp.bfloat16)
    gphi = jnp.einsum('dac,ec->dae', g_bf.astype(jnp.float32), w_o.astype(jnp.float32), precision=lax.Precision.HIGHEST).astype(jnp.bfloat16)
    frac_d = frac.reshape(3, devices, width).transpose(1, 0, 2)
    k_real = k_int.astype(jnp.float32)

    def first_pass(item):
        piece, qd, gd = item
        cosv, sinv = phase_tables(k_real, piece)
        s_loc = jnp.stack([jnp.dot(cosv, qd, preferred_element_type=jnp.float32), jnp.dot(sinv, qd, preferred_element_type=jnp.float32)])
        g_loc = jnp.stack([jnp.dot(cosv, gd, preferred_element_type=jnp.float32), jnp.dot(sinv, gd, preferred_element_type=jnp.float32)])
        return (s_loc, g_loc)
    s_all, g_all = lax.map(first_pass, (frac_d, q_b, gphi))
    s_sum = lax.optimization_barrier(jnp.sum(s_all, axis=0))
    g_sum = lax.optimization_barrier(jnp.sum(g_all, axis=0))
    weights_k = (kernel * (1.0 / math.sqrt(kernel.shape[0] * ATOMS)))[None, :, None]
    coef = (weights_k * s_sum).astype(jnp.bfloat16)
    gcoef = (weights_k * g_sum).astype(jnp.bfloat16)
    contract = (((0,), (0,)), ((), ()))

    def second_pass(piece):
        cosv, sinv = phase_tables(k_real, piece)
        phi = lax.dot_general(cosv, coef[0], contract, preferred_element_type=jnp.float32) + lax.dot_general(sinv, coef[1], contract, preferred_element_type=jnp.float32)
        gq = lax.dot_general(cosv, gcoef[0], contract, preferred_element_type=jnp.float32) + lax.dot_general(sinv, gcoef[1], contract, preferred_element_type=jnp.float32)
        return (phi, gq)
    phi, gq = lax.map(second_pass, frac_d)
    phi_b = jnp.where(live, phi, jnp.float32(0.0)).astype(jnp.bfloat16)
    gq_b = jnp.where(live, gq, jnp.float32(0.0)).astype(jnp.bfloat16)
    grad_h = grad_h + jnp.einsum('dae,ce->dac', gq_b.astype(jnp.float32), w_q.astype(jnp.float32), precision=lax.Precision.HIGHEST)
    gmsg = jnp.einsum('dac,dae->ce', ext.astype(jnp.float32), gu_b.astype(jnp.float32), precision=lax.Precision.HIGHEST)
    gwq = jnp.einsum('dac,dae->ce', hfeat.astype(jnp.float32), gq_b.astype(jnp.float32), precision=lax.Precision.HIGHEST)
    gwo = jnp.einsum('dac,dae->ce', phi_b.astype(jnp.float32), g_bf.astype(jnp.float32), precision=lax.Precision.HIGHEST)
    rad_sum = lax.optimization_barrier(jnp.sum(rad, axis=0))
    rscale = 1.0 / math.sqrt(ATOMS)
    return (grad_h.reshape(ATOMS, chans), gmsg * rscale, rad_sum * (rscale / math.sqrt(NBR)), gwq * rscale, gwo * rscale)
```

```python
import math

import jax
import jax.numpy as jnp
import numpy as np
from jax import lax
from jax.experimental import pallas as pl
from jax.experimental.pallas import tpu as pltpu
from jax.sharding import PartitionSpec as P

MESH = pl.DeviceIdType.MESH
BF = jnp.bfloat16
F32 = jnp.float32

WIDTH, GHOSTS, CHANS, SLOTS, KCOUNT, NB = 512, 128, 128, 64, 1024, 16
BLOCK, WINDOW = 128, 256
X, YZ, CORES = 4, 16, 2
HALF, QUART, PIECE = KCOUNT, KCOUNT // X, KCOUNT // X // YZ
TOTAL = WIDTH * X * YZ * CORES
ROWS_AR = 24


def fitted(fn, degree):
    nodes = (np.cos(np.pi * (np.arange(64) + 0.5) / 64) + 1.0) / 8.0
    series = np.polynomial.chebyshev.Chebyshev.fit(nodes, fn(nodes), degree, domain=[0.0, 0.25])
    return [float(np.float32(c)) for c in series.convert(kind=np.polynomial.Polynomial).coef]


COS = fitted(lambda y: np.cos(2 * np.pi * np.sqrt(y)), 7)
SIN = fitted(lambda y: np.sin(2 * np.pi * np.sqrt(y)) / np.sqrt(y), 6)


def horner(coefs, y):
    value = coefs[-1] * y + coefs[-2]
    for c in coefs[-3::-1]:
        value = value * y + c
    return value


def tn(a, b):
    return lax.dot_general(a, b, (((0,), (0,)), ((), ())), preferred_element_type=F32)


def nt(a, b):
    return lax.dot_general(a, b, (((1,), (1,)), ((), ())), preferred_element_type=F32)


def nn(a, b):
    return jnp.dot(a, b, preferred_element_type=F32)


def transposed(a):
    return jnp.transpose(a.astype(F32)).astype(a.dtype)


def kernel(
    feat, frac, kint, kern, dist, nbr, send, counts, cot, wmsg, wrad, wq, wo,
    gf_out, gmsg_out, rad_out, gwq_out, gwo_out,
    table, sg, sg_b, rc, xs, xs_b, rx, ys, ys_b, ry, ag, pc_t,
    g_b, place_t, out_b, ghost, u_own, u_ghost,
    dz, env, lo_s, code_s, gmat, ymat, gul, gug, radacc, gh_b, back, p_t,
    ar, ar1, ar2, fin, send_sem, recv_sem,
):
    dom, sub = lax.axis_index("dom"), lax.axis_index("sub")
    x, inner = dom // 8, dom % 8
    zhi, core = sub // 2, sub % 2
    yz = inner * 2 + zhi
    flat = dom * 4 + sub

    def by_flat(d):
        return (d // 4, d % 4)

    def by_yz(o):
        idx = (yz + o) % YZ
        return idx, (x * 8 + idx // 2, (idx % 2) * 2 + core)

    def by_x(o):
        idx = (x + o) % X
        return idx, (idx * 8 + inner, sub)

    def by_xc(o):
        idx = (x * 2 + core + o) % 8
        return (idx // 2 * 8 + inner, zhi * 2 + idx % 2)

    other_core = (dom, zhi * 2 + 1 - core)
    upper, lower = by_flat((flat + 1) % 128), by_flat((flat + 127) % 128)

    barrier = pltpu.get_barrier_semaphore()
    greeted = [upper, lower, other_core]
    greeted += [by_x(o)[1] for o in range(1, X)]
    greeted += [by_yz(o)[1] for o in range(1, YZ)]
    greeted += [by_xc(o) for o in (1, 3, 5, 7)]
    greeted += [by_xc(o) for o in (2, 4, 6)]
    for peer in greeted:
        pl.semaphore_signal(barrier, inc=1, device_id=peer, device_id_type=MESH)

    sems = iter(range(128))

    def copy(src, dst, peer):
        at = next(sems)
        return pltpu.make_async_remote_copy(
            src_ref=src, dst_ref=dst, send_sem=send_sem.at[at], recv_sem=recv_sem.at[at],
            device_id=peer, device_id_type=MESH,
        )

    live = lax.broadcasted_iota(jnp.int32, (WIDTH, CHANS), 0) < counts[0]
    g_b[...] = jnp.where(live, cot[...].astype(F32), 0.0).astype(BF)
    picks = jnp.concatenate([send[0:1, :], send[1:2, :]], axis=1)
    place_t[...] = jnp.where(
        lax.broadcasted_iota(jnp.int32, (WIDTH, 2 * GHOSTS), 0) == picks, 1.0, 0.0
    ).astype(BF)
    out_b[...] = tn(place_t[...], feat[...]).astype(BF)

    def table_rows(step, _):
        base = pl.multiple_of(step * 128, 128)
        k_real = kint[:, pl.ds(base, 128)].astype(F32)
        for part in range(4):
            cols = slice(part * 128, part * 128 + 128)
            turns = lax.dot_general(
                k_real, frac[:, cols], (((0,), (0,)), ((), ())),
                precision=lax.Precision.HIGHEST, preferred_element_type=F32,
            )
            turns = turns - jnp.floor(turns + 0.5)
            square = turns * turns
            table[pl.ds(base, 128), cols] = horner(COS, square).astype(BF)
            table[pl.ds(KCOUNT + base, 128), cols] = (horner(SIN, square) * turns).astype(BF)
        return 0

    lax.fori_loop(0, KCOUNT // 128, table_rows, 0)

    def sg_rows(step, _):
        rows = pl.ds(pl.multiple_of(step * 256, 256), 256)
        part = nn(table[rows, :], g_b[...])
        sg[rows, :] = part
        sg_b[rows, :] = part.astype(BF)
        return 0

    lax.fori_loop(0, 2 * KCOUNT // 256, sg_rows, 0)

    pl.semaphore_wait(barrier, len(greeted))

    halo = [
        copy(out_b.at[pl.ds(0, GHOSTS)], ghost.at[pl.ds(GHOSTS, GHOSTS)], lower),
        copy(out_b.at[pl.ds(GHOSTS, GHOSTS)], ghost.at[pl.ds(0, GHOSTS)], upper),
    ]
    cores = copy(sg_b.at[pl.ds(pl.multiple_of((1 - core) * HALF, HALF), HALF)], rc, other_core)
    for c in halo + [cores]:
        c.start()

    def spread_block(blk):
        w = min(max(blk * BLOCK - BLOCK // 2, 0), WIDTH - WINDOW)
        half = BLOCK // 2
        first, second = slice(blk * BLOCK, blk * BLOCK + half), slice(blk * BLOCK + half, (blk + 1) * BLOCK)
        d2 = jnp.concatenate([dist[first, :], dist[second, :]], axis=1)
        n2 = jnp.concatenate([nbr[first, :], nbr[second, :]], axis=1)
        dz[...] = d2 * (1.0 / 0.4)
        env[...] = jnp.square(jnp.maximum(0.0, 1.0 - d2 * (1.0 / 6.0)))
        place = jnp.where(n2 >= WIDTH, n2 - (WIDTH - WINDOW), n2 - w)
        lane = lax.broadcasted_iota(jnp.int32, (half, 128), 1)
        lo_s[...] = (place & 127).astype(F32)
        code_s[...] = ((place >> 7) + jnp.where(lane >= SLOTS, 4, 0)).astype(F32)

        def group(step, _):
            base = pl.multiple_of(step * 8, 8)
            rows = pl.ds(base, 8)
            dz8, env8, lo8, code8 = dz[rows, :], env[rows, :], lo_s[rows, :], code_s[rows, :]
            b_ids = lax.broadcasted_iota(jnp.int32, (NB, 128), 0).astype(F32)
            lo_ids = lax.broadcasted_iota(jnp.int32, (128, 128), 0).astype(F32).astype(BF)
            for s in range(8):
                z = dz8[s : s + 1, :] - b_ids
                basis = (jnp.exp(-(z * z)) * env8[s : s + 1, :]).astype(BF)
                code = jnp.broadcast_to(code8[s : s + 1, :], (NB, 128)).astype(BF)
                lhs = jnp.concatenate(
                    [jnp.where(code == h, basis, jnp.zeros_like(basis)) for h in range(8)], axis=0
                )
                lo = jnp.broadcast_to(lo8[s : s + 1, :], (128, 128)).astype(BF)
                hot = jnp.where(lo_ids == lo, jnp.ones_like(lo), jnp.zeros_like(lo))
                out = nt(lhs, hot).astype(BF)
                for i in range(2):
                    at = pl.multiple_of((blk * BLOCK + i * half + s) * NB + base * NB, NB)
                    for h in range(4):
                        r = (i * 4 + h) * NB
                        gmat[pl.ds(at, NB), h * 128 : h * 128 + 128] = out[r : r + NB, :]
            return 0

        lax.fori_loop(0, half // 8, group, 0)

    spread_block(0)

    cores.wait()
    mine = pl.multiple_of(core * HALF, HALF)

    def add_core(step, _):
        rows = pl.ds(pl.multiple_of(step * 128, 128), 128)
        val = sg[pl.ds(pl.multiple_of(mine + step * 128, 128), 128), :] + rc[rows, :].astype(F32)
        xs[rows, :] = val
        xs_b[rows, :] = val.astype(BF)
        return 0

    lax.fori_loop(0, HALF // 128, add_core, 0)
    along_x = []
    for o in range(1, X):
        idx, peer = by_x(o)
        along_x.append(copy(xs_b.at[pl.ds(pl.multiple_of(idx * QUART, QUART), QUART)], rx.at[o - 1], peer))
    for c in along_x:
        c.start()

    spread_block(1)

    for c in along_x:
        c.wait()
    val = xs[pl.ds(pl.multiple_of(x * QUART, QUART), QUART), :]
    for o in range(1, X):
        val = val + rx[o - 1].astype(F32)
    ys[...] = val
    ys_b[...] = val.astype(BF)
    along_yz = []
    for o in range(1, YZ):
        idx, peer = by_yz(o)
        along_yz.append(copy(ys_b.at[pl.ds(pl.multiple_of(idx * PIECE, PIECE), PIECE)], ry.at[o - 1], peer))
    for c in along_yz:
        c.start()

    spread_block(2)

    for c in along_yz:
        c.wait()
    val = ys[pl.ds(pl.multiple_of(yz * PIECE, PIECE), PIECE), :]
    for o in range(1, YZ):
        val = val + ry[o - 1].astype(F32)
    at_piece = pl.ds(pl.multiple_of(core * HALF + x * QUART + yz * PIECE, PIECE), PIECE)
    at_quart = pl.ds(pl.multiple_of(core * HALF + x * QUART, QUART), QUART)
    at_half = pl.ds(mine, HALF)
    ag[at_piece, :] = val.astype(BF)
    gather_yz = [copy(ag.at[at_piece], ag.at[at_piece], by_yz(o)[1]) for o in range(1, YZ)]
    for c in gather_yz:
        c.start()

    spread_block(3)

    for c in gather_yz:
        c.wait()
    gather_x = [copy(ag.at[at_quart], ag.at[at_quart], by_x(o)[1]) for o in range(1, X)]
    for c in gather_x:
        c.start()

    for c in halo:
        c.wait()
    u_own[...] = nn(feat[...], wmsg[...]).astype(BF)
    u_ghost[...] = nn(ghost[...], wmsg[...]).astype(BF)
    gul[...] = jnp.zeros_like(gul)
    gug[...] = jnp.zeros_like(gug)
    radacc[...] = jnp.zeros_like(radacc)
    wr = wrad[...].astype(F32)

    def edge_block(blk, _):
        w = pl.multiple_of(jnp.clip(blk * BLOCK - BLOCK // 2, 0, WIDTH - WINDOW), 64)
        u_win = u_own[pl.ds(w, WINDOW), :]
        ug = u_ghost[...]
        piece = 32

        def atoms(step, _):
            at = pl.multiple_of(blk * BLOCK + step * piece, piece)
            rows = pl.ds(pl.multiple_of(at * NB, NB * piece), NB * piece)
            summed = nn(gmat[rows, :WINDOW], u_win) + nn(gmat[rows, WINDOW:], ug)
            summed = summed.reshape(piece, NB, CHANS)
            pre = jnp.sum(summed * wr[None], axis=1)
            sig = 1.0 / (1.0 + jnp.exp(-pre))
            gpre = g_b[pl.ds(at, piece), :].astype(F32) * sig * (1.0 + pre * (1.0 - sig))
            wide = gpre[:, None, :]
            radacc[...] += jnp.sum(wide * summed, axis=0)
            ymat[pl.ds(pl.multiple_of(step * piece * NB, NB * piece), NB * piece), :] = (
                (wide * wr[None]).reshape(piece * NB, CHANS).astype(BF)
            )
            return 0

        lax.fori_loop(0, BLOCK // piece, atoms, 0)
        rows = pl.ds(pl.multiple_of(blk * BLOCK * NB, BLOCK * NB), BLOCK * NB)
        collected = jnp.transpose(tn(ymat[...], gmat[rows, :]))
        gul[pl.ds(w, WINDOW), :] += collected[:WINDOW, :]
        gug[...] += collected[WINDOW:, :]
        return 0

    edge_block(0, 0)
    for c in gather_x:
        c.wait()
    gather_core = copy(ag.at[at_half], ag.at[at_half], other_core)
    gather_core.start()
    lax.fori_loop(1, WIDTH // BLOCK, edge_block, 0)

    gu_g = gug[...].astype(BF)
    gu_l = gul[...].astype(BF)
    gh_b[...] = nt(gu_g, wmsg[...]).astype(BF)
    returns = [
        copy(gh_b.at[pl.ds(0, GHOSTS)], back.at[pl.ds(GHOSTS, GHOSTS)], lower),
        copy(gh_b.at[pl.ds(GHOSTS, GHOSTS)], back.at[pl.ds(0, GHOSTS)], upper),
    ]
    for c in returns:
        c.start()
    gmsg = tn(feat[...], gu_l) + tn(ghost[...], gu_g)

    gather_core.wait()

    def flip(step, _):
        base = pl.multiple_of(step * 128, 128)
        weight = kern[:, pl.ds(pl.multiple_of((step % 8) * 128, 128), 128)]
        part = jnp.transpose(ag[pl.ds(base, 128), :].astype(F32))
        pc_t[:, pl.ds(base, 128)] = (part * (weight * (1.0 / math.sqrt(KCOUNT * TOTAL)))).astype(BF)
        return 0

    lax.fori_loop(0, 2 * KCOUNT // 128, flip, 0)
    p_t[...] = nn(pc_t[...], table[...]).astype(BF)
    f_live = jnp.where(live, feat[...].astype(F32), 0.0).astype(BF)
    m_t = nn(p_t[...], f_live)

    ar[:, 0:8, :] = gmsg.reshape(YZ, 8, CHANS)
    ar[:, 8:16, :] = m_t.reshape(YZ, 8, CHANS)
    ar[:, 16:24, :] = jnp.zeros((YZ, 8, CHANS), F32)
    for j in range(YZ):
        ar[j, 16:17, :] = radacc[j : j + 1, :]
    ar_yz = []
    for o in range(1, YZ):
        idx, peer = by_yz(o)
        ar_yz.append(copy(ar.at[idx], ar1.at[o - 1], peer))
    for c in ar_yz:
        c.start()

    gq_t = nn(wo[...], p_t[...]).astype(BF)
    ghq = jnp.transpose(nn(wq[...], gq_t))
    base_grad = g_b[...].astype(F32) + nt(gu_l, wmsg[...]) + jnp.where(live, ghq, 0.0)
    for c in returns:
        c.wait()
    gf_out[...] = base_grad + nn(place_t[...], back[...])

    for c in ar_yz:
        c.wait()
    val = ar[yz]
    for o in range(1, YZ):
        val = val + ar1[o - 1]
    me = x * 2 + core
    ar2[me] = val
    ar_xc = [copy(ar2.at[me], ar2.at[me], by_xc(o)) for o in range(1, 8)]
    for c in ar_xc:
        c.start()
    for c in ar_xc:
        c.wait()
    val = ar2[0]
    for j in range(1, 8):
        val = val + ar2[j]
    fin[yz] = val
    ar_fin = [copy(fin.at[yz], fin.at[yz], by_yz(o)[1]) for o in range(1, YZ)]
    for c in ar_fin:
        c.start()
    for c in ar_fin:
        c.wait()

    rscale = 1.0 / math.sqrt(TOTAL)
    gmsg_out[...] = fin[:, 0:8, :].reshape(CHANS, CHANS) * rscale
    for j in range(NB):
        rad_out[j : j + 1, :] = fin[j, 16:17, :] * (rscale / math.sqrt(SLOTS))
    m_full = jnp.transpose(fin[:, 8:16, :].reshape(CHANS, CHANS))
    m_hi = m_full.astype(BF)
    m_lo = (m_full - m_hi.astype(F32)).astype(BF)
    gwq_out[...] = (nt(m_hi, wo[...]) + nt(m_lo, wo[...])) * rscale
    wq_t = transposed(wq[...])
    gwo_out[...] = (nn(wq_t, m_hi) + nn(wq_t, m_lo)) * rscale


def on_device(features, frac, k_int, kern, dist, nbr, send_index, counts, cot, w_msg, w_rad, w_q, w_o):
    vmem = pl.BlockSpec(memory_space=pltpu.VMEM)
    smem = pl.BlockSpec(memory_space=pltpu.SMEM)

    def buf(*shape, dtype=BF):
        return pltpu.VMEM(shape, dtype)

    return pl.pallas_call(
        kernel,
        out_shape=(
            jax.ShapeDtypeStruct((WIDTH, CHANS), F32),
            jax.ShapeDtypeStruct((CHANS, CHANS), F32),
            jax.ShapeDtypeStruct((NB, CHANS), F32),
            jax.ShapeDtypeStruct((CHANS, CHANS), F32),
            jax.ShapeDtypeStruct((CHANS, CHANS), F32),
        ),
        in_specs=[vmem] * 7 + [smem] + [vmem] * 5,
        out_specs=(vmem,) * 5,
        scratch_shapes=[
            buf(2 * KCOUNT, WIDTH),
            buf(2 * KCOUNT, CHANS, dtype=F32),
            buf(2 * KCOUNT, CHANS),
            buf(HALF, CHANS),
            buf(HALF, CHANS, dtype=F32),
            buf(HALF, CHANS),
            buf(X - 1, QUART, CHANS),
            buf(QUART, CHANS, dtype=F32),
            buf(QUART, CHANS),
            buf(YZ - 1, PIECE, CHANS),
            buf(2 * KCOUNT, CHANS),
            buf(CHANS, 2 * KCOUNT),
            buf(WIDTH, CHANS),
            buf(WIDTH, 2 * GHOSTS),
            buf(2 * GHOSTS, CHANS),
            buf(2 * GHOSTS, CHANS),
            buf(WIDTH, CHANS),
            buf(2 * GHOSTS, CHANS),
            buf(BLOCK // 2, 128, dtype=F32),
            buf(BLOCK // 2, 128, dtype=F32),
            buf(BLOCK // 2, 128, dtype=F32),
            buf(BLOCK // 2, 128, dtype=F32),
            buf(WIDTH * NB, 2 * WINDOW),
            buf(BLOCK * NB, CHANS),
            buf(WIDTH, CHANS, dtype=F32),
            buf(2 * GHOSTS, CHANS, dtype=F32),
            buf(NB, CHANS, dtype=F32),
            buf(2 * GHOSTS, CHANS),
            buf(2 * GHOSTS, CHANS),
            buf(CHANS, WIDTH),
            buf(YZ, ROWS_AR, CHANS, dtype=F32),
            buf(YZ - 1, ROWS_AR, CHANS, dtype=F32),
            buf(8, ROWS_AR, CHANS, dtype=F32),
            buf(YZ, ROWS_AR, CHANS, dtype=F32),
            pltpu.SemaphoreType.DMA((96,)),
            pltpu.SemaphoreType.DMA((96,)),
        ],
        compiler_params=pltpu.CompilerParams(
            collective_id=0, has_side_effects=True, vmem_limit_bytes=48 * 1024 * 1024
        ),
        name="ewald_backward",
    )(
        features, frac, k_int, kern.reshape(1, KCOUNT), dist, nbr,
        send_index.reshape(2, GHOSTS), counts, cot, w_msg, w_rad, w_q, w_o,
    )


def solution(mesh):
    rows = P(("dom", "sub"), None)
    placed = (
        rows, P(None, ("dom", "sub")), P(), P(), rows, rows,
        P(("dom", "sub"), None, None), P(("dom", "sub")), rows, P(), P(), P(), P(),
    )
    return jax.shard_map(
        on_device,
        mesh=mesh,
        in_specs=placed,
        out_specs=(rows, P(), P(), P(), P()),
        check_vma=False,
    )
```

```python
import math

import jax
import jax.numpy as jnp
import numpy as np
from jax import lax
from jax.experimental import pallas as pl
from jax.experimental.pallas import tpu as pltpu
from jax.sharding import PartitionSpec as P

MESH = pl.DeviceIdType.MESH
BF = jnp.bfloat16
F32 = jnp.float32

WIDTH, GHOSTS, CHANS, SLOTS, KCOUNT, NB = 512, 128, 128, 64, 1024, 16
BLOCK, WINDOW = 128, 256
X, YZ, CORES = 4, 16, 2
CHIPS = X * YZ
PIECE = KCOUNT // CHIPS
TOTAL = WIDTH * CHIPS * CORES
BOTH = 2 * CHANS
ROWS_AR = 24
VMEM_BYTES = 63 * 1024 * 1024


def fitted(fn, degree):
    nodes = (np.cos(np.pi * (np.arange(64) + 0.5) / 64) + 1.0) / 8.0
    series = np.polynomial.chebyshev.Chebyshev.fit(nodes, fn(nodes), degree, domain=[0.0, 0.25])
    return [float(np.float32(c)) for c in series.convert(kind=np.polynomial.Polynomial).coef]


COS = fitted(lambda y: np.cos(2 * np.pi * np.sqrt(y)), 6)
SIN = fitted(lambda y: np.sin(2 * np.pi * np.sqrt(y)) / np.sqrt(y), 5)


def horner(coefs, y):
    value = coefs[-1] * y + coefs[-2]
    for c in coefs[-3::-1]:
        value = value * y + c
    return value


def tn(a, b):
    return lax.dot_general(a, b, (((0,), (0,)), ((), ())), preferred_element_type=F32)


def nt(a, b):
    return lax.dot_general(a, b, (((1,), (1,)), ((), ())), preferred_element_type=F32)


def nn(a, b):
    return jnp.dot(a, b, preferred_element_type=F32)


def transposed(a):
    return jnp.transpose(a.astype(F32)).astype(a.dtype)


def kernel(
    feat_h, frac_h, kint_h, kern_h, dist_h, nbr_h, send_h, counts_h, cot_h, wmsg_h, wrad_h, wq_h, wo_h,
    gf_out, gmsg_out, rad_out, gwq_out, gwo_out,
    feat, frac, kint, kern, dist, nbr, send, counts, cot, wmsg, wrad, wq, wo,
    gf, gmsg_s, rad_s, gwq, gwo,
    table, sg_b, rc, xs, xs_b, rx, ag, pc_t,
    fg, place_t, out_b, ghost, u_own, u_ghost,
    dz, env, lo_s, code_s, gmat, ymat, gul, gug, radacc, gh_b, back, p_t, m_s,
    ar, ar1, ar2, fin, in_sem, out_sem, send_sem, recv_sem, rs_send, rs_recv, ag_send, ag_recv,
):
    dom, sub = lax.axis_index("dom"), lax.axis_index("sub")
    x, zlo, y = dom // 8, (dom // 4) % 2, dom % 4
    zhi, core = sub // 2, sub % 2
    z = zhi * 2 + zlo
    yz = y * 4 + z
    chip = x * YZ + yz
    flat = dom * 4 + sub

    px = [(x + d) % 4 for d in range(4)]
    py = [(y + d) % 4 for d in range(4)]
    pz = [(z + d) % 4 for d in range(4)]
    far = [p * 8 for p in px]
    along = [(p % 2) * 4 for p in pz]
    pair_of = [(p // 2) * 2 for p in pz]
    both_cores = [core, 1 - core]

    def shifted(dx, dy, dz_, dc=0):
        where = (far[dx] + (along[dz_] + py[dy]), pair_of[dz_] + both_cores[dc])
        return px[dx] * YZ + (py[dy] * 4 + pz[dz_]), where

    def hops(turn):
        return sum(min(d, 4 - d) for d in turn)

    turns = [(a, b, c) for a in range(4) for b in range(4) for c in range(4) if a or b or c]
    turns = sorted(turns, key=lambda t: -hops(t))
    places = [shifted(*t) for t in turns]
    plane = [(t, p) for t, p in zip(turns, places) if not t[0]]

    other_core = (dom, zhi * 2 + 1 - core)
    upper, lower = (flat + 1) % 128, (flat + 127) % 128
    upper, lower = (upper // 4, upper % 4), (lower // 4, lower % 4)
    across = [(dx, dc) for dx in (2, 1, 3, 0) for dc in (1, 0) if dx or dc]
    across = [shifted(dx, 0, 0, dc)[1] for dx, dc in across]

    barrier = pltpu.get_barrier_semaphore()

    def greet(peer):
        pl.semaphore_signal(barrier, inc=1, device_id=peer, device_id_type=MESH)

    for _, peer in places:
        greet(peer)
    for peer in (upper, lower, other_core):
        greet(peer)
    for dx in range(1, X):
        greet(shifted(dx, 0, 0, 1)[1])
    greeted = CHIPS - 1 + 3 + X - 1

    sems = iter(range(128))

    def copy(src, dst, peer):
        at = next(sems)
        return pltpu.make_async_remote_copy(
            src_ref=src, dst_ref=dst, send_sem=send_sem.at[at], recv_sem=recv_sem.at[at],
            device_id=peer, device_id_type=MESH,
        )

    pairs = [
        (counts_h, counts), (kint_h, kint), (frac_h, frac), (feat_h, feat), (cot_h, cot), (send_h, send),
        (dist_h, dist), (nbr_h, nbr), (wmsg_h, wmsg), (wrad_h, wrad), (kern_h, kern), (wq_h, wq), (wo_h, wo),
    ]
    loads = [pltpu.make_async_copy(src, dst, in_sem.at[i]) for i, (src, dst) in enumerate(pairs)]
    for c in loads:
        c.start()
    for c in loads:
        c.wait()

    live = lax.broadcasted_iota(jnp.int32, (WIDTH, CHANS), 0) < counts[0]
    fg[:, :CHANS] = jnp.where(live, feat[...].astype(F32), 0.0).astype(BF)
    fg[:, CHANS:] = jnp.where(live, cot[...].astype(F32), 0.0).astype(BF)
    picks = jnp.concatenate([send[0:1, :], send[1:2, :]], axis=1)
    place_t[...] = jnp.where(
        lax.broadcasted_iota(jnp.int32, (WIDTH, 2 * GHOSTS), 0) == picks, 1.0, 0.0
    ).astype(BF)
    out_b[...] = tn(place_t[...], feat[...]).astype(BF)

    def table_rows(step, _):
        base = pl.multiple_of(step * 128, 128)
        k_real = kint[:, pl.ds(base, 128)].astype(F32)
        for part in range(4):
            cols = slice(part * 128, part * 128 + 128)
            turns = lax.dot_general(
                k_real, frac[:, cols], (((0,), (0,)), ((), ())),
                precision=lax.Precision.HIGHEST, preferred_element_type=F32,
            )
            turns = turns - jnp.floor(turns + 0.5)
            square = turns * turns
            table[pl.ds(base, 128), cols] = horner(COS, square).astype(BF)
            table[pl.ds(KCOUNT + base, 128), cols] = (horner(SIN, square) * turns).astype(BF)
        return 0

    lax.fori_loop(0, KCOUNT // 128, table_rows, 0)

    theirs = pl.multiple_of((1 - core) * KCOUNT, KCOUNT)
    mine = pl.multiple_of(core * KCOUNT, KCOUNT)
    sg_b[...] = nn(table[pl.ds(theirs, KCOUNT), :], fg[...]).astype(BF)
    xs[...] = nn(table[pl.ds(mine, KCOUNT), :], fg[...])

    pl.semaphore_wait(barrier, greeted)

    halo = [
        copy(out_b.at[pl.ds(0, GHOSTS)], ghost.at[pl.ds(GHOSTS, GHOSTS)], lower),
        copy(out_b.at[pl.ds(GHOSTS, GHOSTS)], ghost.at[pl.ds(0, GHOSTS)], upper),
    ]
    cores = copy(sg_b, rc, other_core)
    for c in [cores] + halo:
        c.start()

    def spread_setup(pair):
        blocks = (2 * pair, 2 * pair + 1)
        d_parts, p_parts = [], []
        for i, blk in enumerate(blocks):
            w = min(max(blk * BLOCK - BLOCK // 2, 0), WIDTH - WINDOW)
            cols = slice(blk * BLOCK, (blk + 1) * BLOCK)
            n = nbr[:, cols]
            d_parts.append(dist[:, cols])
            place = jnp.where(n >= WIDTH, n - (WIDTH - WINDOW), n - w) + i * 2 * WINDOW
            p_parts.append(place.astype(F32))
        d2 = jnp.transpose(jnp.concatenate(d_parts, axis=0))
        place = jnp.transpose(jnp.concatenate(p_parts, axis=0))
        dz[...] = d2 * (1.0 / 0.4)
        env[...] = jnp.square(jnp.maximum(0.0, 1.0 - d2 * (1.0 / 6.0)))
        code = jnp.floor(place * (1.0 / 128.0))
        lo_s[...] = place - code * 128.0
        code_s[...] = code

    def spread_blocks(pair, first, last):
        blocks = (2 * pair, 2 * pair + 1)

        def group(step, _):
            base = pl.multiple_of(step * 8, 8)
            rows = pl.ds(base, 8)
            dz8, env8, lo8, code8 = dz[rows, :], env[rows, :], lo_s[rows, :], code_s[rows, :]
            b_ids = lax.broadcasted_iota(jnp.int32, (NB, 128), 0).astype(F32)
            lo_ids = lax.broadcasted_iota(jnp.int32, (128, 128), 0).astype(F32).astype(BF)
            for s in range(8):
                gap = dz8[s : s + 1, :] - b_ids
                basis = (jnp.exp(-(gap * gap)) * env8[s : s + 1, :]).astype(BF)
                code = jnp.broadcast_to(code8[s : s + 1, :], (NB, 128)).astype(BF)
                lhs = jnp.concatenate(
                    [jnp.where(code == h, basis, jnp.zeros_like(basis)) for h in range(8)], axis=0
                )
                lo = jnp.broadcast_to(lo8[s : s + 1, :], (128, 128)).astype(BF)
                hot = jnp.where(lo_ids == lo, jnp.ones_like(lo), jnp.zeros_like(lo))
                out = nt(lhs, hot).astype(BF)
                for i in range(2):
                    at = pl.multiple_of((blocks[i] * BLOCK + s) * NB + base * NB, NB)
                    for h in range(4):
                        r = (i * 4 + h) * NB
                        gmat[pl.ds(at, NB), h * 128 : h * 128 + 128] = out[r : r + NB, :]
            return 0

        lax.fori_loop(first, last, group, 0)

    spread_setup(0)
    spread_blocks(0, 0, 8)

    cores.wait()

    def add_core(step, _):
        rows = pl.ds(pl.multiple_of(step * 64, 64), 64)
        val = xs[rows, :] + rc[rows, :].astype(F32)
        xs[rows, :] = val
        xs_b[rows, :] = val.astype(BF)
        return 0

    lax.fori_loop(0, KCOUNT // 64, add_core, 0)

    scatters = [
        pltpu.make_async_remote_copy(
            src_ref=xs_b.at[pl.ds(pl.multiple_of(to * PIECE, PIECE), PIECE)], dst_ref=rx.at[i],
            send_sem=rs_send.at[i], recv_sem=rs_recv.at[i], device_id=peer, device_id_type=MESH,
        )
        for i, (to, peer) in enumerate(places)
    ]
    for c in scatters:
        c.start()

    spread_blocks(0, 8, 16)
    spread_setup(1)
    spread_blocks(1, 0, 16)

    for c in scatters:
        c.wait()
    own = xs[pl.ds(pl.multiple_of(chip * PIECE, PIECE), PIECE), :]
    own = lax.fori_loop(0, CHIPS - 1, lambda i, v: v + rx[i].astype(F32), own)
    at_piece = pl.ds(pl.multiple_of(mine + chip * PIECE, PIECE), PIECE)
    at_half = pl.ds(mine, KCOUNT)
    ag[at_piece, :] = own.astype(BF)
    gathers = [
        pltpu.make_async_remote_copy(
            src_ref=ag.at[at_piece], dst_ref=ag.at[at_piece],
            send_sem=ag_send.at[i], recv_sem=ag_recv.at[i], device_id=peer, device_id_type=MESH,
        )
        for i, (_, peer) in enumerate(places)
    ]
    for c in gathers:
        c.start()

    for c in halo:
        c.wait()
    u_own[...] = nn(feat[...], wmsg[...]).astype(BF)
    u_ghost[...] = nn(ghost[...], wmsg[...]).astype(BF)
    gul[...] = jnp.zeros_like(gul)
    gug[...] = jnp.zeros_like(gug)
    radacc[...] = jnp.zeros_like(radacc)
    wr = wrad[...].astype(F32)

    def edge_block(blk, _):
        w = pl.multiple_of(jnp.clip(blk * BLOCK - BLOCK // 2, 0, WIDTH - WINDOW), 64)
        u_win = u_own[pl.ds(w, WINDOW), :]
        ug = u_ghost[...]
        piece = 32

        def atoms(step, _):
            at = pl.multiple_of(blk * BLOCK + step * piece, piece)
            rows = pl.ds(pl.multiple_of(at * NB, NB * piece), NB * piece)
            summed = nn(gmat[rows, :WINDOW], u_win) + nn(gmat[rows, WINDOW:], ug)
            summed = summed.reshape(piece, NB, CHANS)
            pre = jnp.sum(summed * wr[None], axis=1)
            sig = 1.0 / (1.0 + jnp.exp(-pre))
            gpre = fg[pl.ds(at, piece), CHANS:].astype(F32) * sig * (1.0 + pre * (1.0 - sig))
            wide = gpre[:, None, :]
            radacc[...] += jnp.sum(wide * summed, axis=0)
            ymat[pl.ds(pl.multiple_of(step * piece * NB, NB * piece), NB * piece), :] = (
                (wide * wr[None]).reshape(piece * NB, CHANS).astype(BF)
            )
            return 0

        lax.fori_loop(0, BLOCK // piece, atoms, 0)
        rows = pl.ds(pl.multiple_of(blk * BLOCK * NB, BLOCK * NB), BLOCK * NB)
        collected = jnp.transpose(tn(ymat[...], gmat[rows, :]))
        gul[pl.ds(w, WINDOW), :] += collected[:WINDOW, :]
        gug[...] += collected[WINDOW:, :]
        return 0

    lax.fori_loop(0, WIDTH // BLOCK, edge_block, 0)

    gu_g = gug[...].astype(BF)
    gu_l = gul[...].astype(BF)
    gmsg = tn(feat[...], gu_l) + tn(ghost[...], gu_g)

    ar[:, 0:16, :] = gmsg.reshape(8, 16, CHANS)
    ar[:, 16:24, :] = jnp.zeros((8, 8, CHANS), F32)
    for j in range(8):
        ar[j, 16:18, :] = radacc[2 * j : 2 * j + 2, :]
    me = x * 2 + core
    ar_first = []
    for o, peer in enumerate(across):
        ar_first.append(copy(ar.at[lax.rem(peer[0], 32) // 8 * 2 + lax.rem(peer[1], 2)], ar1.at[o], peer))
    for c in ar_first:
        c.start()

    gh_b[...] = nt(gu_g, wmsg[...]).astype(BF)
    returns = [
        copy(gh_b.at[pl.ds(0, GHOSTS)], back.at[pl.ds(GHOSTS, GHOSTS)], lower),
        copy(gh_b.at[pl.ds(GHOSTS, GHOSTS)], back.at[pl.ds(0, GHOSTS)], upper),
    ]
    for c in returns:
        c.start()

    gul[...] = fg[:, CHANS:].astype(F32) + nt(gu_l, wmsg[...])

    for c in gathers:
        c.wait()
    gather_core = copy(ag.at[at_half], ag.at[at_half], other_core)
    gather_core.start()

    def half_of(start, which):
        def flip(step, _):
            at = pl.multiple_of(step * 128, 128)
            base = pl.multiple_of(start + at, 128)
            part = jnp.transpose(ag[pl.ds(base, 128), CHANS:].astype(F32))
            weight = kern[:, pl.ds(at, 128)] * (1.0 / math.sqrt(KCOUNT * TOTAL))
            pc_t[:, pl.ds(at, 128)] = (part * weight).astype(BF)
            return 0

        lax.fori_loop(0, KCOUNT // 128, flip, 0)
        rows = pl.ds(start, KCOUNT)
        m_s[which] = nn(pc_t[...], ag[rows, :CHANS])
        return nn(pc_t[...], table[rows, :])

    p_t[...] = half_of(mine, core)

    for c in ar_first:
        c.wait()
    val = ar[me]
    for o in range(7):
        val = val + ar1[o]
    ar2[yz] = val
    ar_yz = [copy(ar2.at[yz], ar2.at[yz], peer) for _, (_, peer) in plane]
    for c in ar_yz:
        c.start()

    gather_core.wait()
    p_b = (p_t[...] + half_of(theirs, 1 - core)).astype(BF)
    gq_t = nn(wo[...], p_b).astype(BF)
    ghq = jnp.transpose(nn(wq[...], gq_t))
    base_grad = gul[...] + jnp.where(live, ghq, 0.0)
    for c in returns:
        c.wait()
    gf[...] = base_grad + nn(place_t[...], back[...])
    outs = [
        pltpu.make_async_copy(src, dst, out_sem.at[i])
        for i, (src, dst) in enumerate(
            [(gf, gf_out), (gwq, gwq_out), (gwo, gwo_out), (gmsg_s, gmsg_out), (rad_s, rad_out)]
        )
    ]
    outs[0].start()

    rscale = 1.0 / math.sqrt(TOTAL)
    m_full = jnp.transpose(m_s[0] + m_s[1])
    m_hi = m_full.astype(BF)
    m_lo = (m_full - m_hi.astype(F32)).astype(BF)
    gwq[...] = (nt(m_hi, wo[...]) + nt(m_lo, wo[...])) * rscale
    wq_t = transposed(wq[...])
    gwo[...] = (nn(wq_t, m_hi) + nn(wq_t, m_lo)) * rscale
    outs[1].start()
    outs[2].start()

    for c in ar_yz:
        c.wait()
    val = ar2[0]
    for j in range(1, YZ):
        val = val + ar2[j]
    fin[me] = val
    ar_fin = [copy(fin.at[me], fin.at[me], peer) for peer in across]
    for c in ar_fin:
        c.start()
    for c in ar_fin:
        c.wait()
    gmsg_s[...] = fin[:, 0:16, :].reshape(CHANS, CHANS) * rscale
    outs[3].start()
    for j in range(8):
        rad_s[2 * j : 2 * j + 2, :] = fin[j, 16:18, :] * (rscale / math.sqrt(SLOTS))
    outs[4].start()
    for c in outs:
        c.wait()


def finish(*refs):
    ins, outs, held, sem = refs[:5], refs[5:10], refs[10:15], refs[15]
    reads = [pltpu.make_async_copy(ins[i], held[i], sem.at[i]) for i in range(5)]
    writes = [pltpu.make_async_copy(held[i], outs[i], sem.at[5 + i]) for i in range(5)]
    for r in reads:
        r.start()
    for r, w in zip(reads, writes):
        r.wait()
        w.start()
    for w in writes:
        w.wait()


def on_device(features, frac, k_int, kern, dist, nbr, send_index, counts, cot, w_msg, w_rad, w_q, w_o):
    hbm = pl.BlockSpec(memory_space=pltpu.HBM)

    def buf(*shape, dtype=BF):
        return pltpu.VMEM(shape, dtype)

    def result(*shape):
        return jax.ShapeDtypeStruct(shape, F32)

    shapes = (result(WIDTH, CHANS), result(CHANS, CHANS), result(NB, CHANS), result(CHANS, CHANS), result(CHANS, CHANS))
    sums = pl.pallas_call(
        kernel,
        out_shape=shapes,
        in_specs=[hbm] * 13,
        out_specs=(hbm,) * 5,
        scratch_shapes=[
            buf(WIDTH, CHANS),
            buf(3, WIDTH, dtype=F32),
            buf(3, KCOUNT, dtype=jnp.int32),
            buf(1, KCOUNT, dtype=F32),
            buf(SLOTS, WIDTH, dtype=F32),
            buf(SLOTS, WIDTH, dtype=jnp.int32),
            buf(2, GHOSTS, dtype=jnp.int32),
            pltpu.SMEM((1,), jnp.int32),
            buf(WIDTH, CHANS),
            buf(CHANS, CHANS),
            buf(NB, CHANS),
            buf(CHANS, CHANS),
            buf(CHANS, CHANS),
            buf(WIDTH, CHANS, dtype=F32),
            buf(CHANS, CHANS, dtype=F32),
            buf(NB, CHANS, dtype=F32),
            buf(CHANS, CHANS, dtype=F32),
            buf(CHANS, CHANS, dtype=F32),
            buf(2 * KCOUNT, WIDTH),
            buf(KCOUNT, BOTH),
            buf(KCOUNT, BOTH),
            buf(KCOUNT, BOTH, dtype=F32),
            buf(KCOUNT, BOTH),
            buf(CHIPS - 1, PIECE, BOTH),
            buf(2 * KCOUNT, BOTH),
            buf(CHANS, KCOUNT),
            buf(WIDTH, BOTH),
            buf(WIDTH, 2 * GHOSTS),
            buf(2 * GHOSTS, CHANS),
            buf(2 * GHOSTS, CHANS),
            buf(WIDTH, CHANS),
            buf(2 * GHOSTS, CHANS),
            buf(BLOCK, 128, dtype=F32),
            buf(BLOCK, 128, dtype=F32),
            buf(BLOCK, 128, dtype=F32),
            buf(BLOCK, 128, dtype=F32),
            buf(WIDTH * NB, 2 * WINDOW),
            buf(BLOCK * NB, CHANS),
            buf(WIDTH, CHANS, dtype=F32),
            buf(2 * GHOSTS, CHANS, dtype=F32),
            buf(NB, CHANS, dtype=F32),
            buf(2 * GHOSTS, CHANS),
            buf(2 * GHOSTS, CHANS),
            buf(CHANS, WIDTH, dtype=F32),
            buf(2, CHANS, CHANS, dtype=F32),
            buf(8, ROWS_AR, CHANS, dtype=F32),
            buf(7, ROWS_AR, CHANS, dtype=F32),
            buf(YZ, ROWS_AR, CHANS, dtype=F32),
            buf(8, ROWS_AR, CHANS, dtype=F32),
            pltpu.SemaphoreType.DMA((13,)),
            pltpu.SemaphoreType.DMA((5,)),
            pltpu.SemaphoreType.DMA((40,)),
            pltpu.SemaphoreType.DMA((40,)),
            pltpu.SemaphoreType.DMA((CHIPS - 1,)),
            pltpu.SemaphoreType.DMA((CHIPS - 1,)),
            pltpu.SemaphoreType.DMA((CHIPS - 1,)),
            pltpu.SemaphoreType.DMA((CHIPS - 1,)),
        ],
        compiler_params=pltpu.CompilerParams(
            collective_id=0, has_side_effects=True, vmem_limit_bytes=VMEM_BYTES
        ),
        name="ewald_backward",
    )(
        features, frac, k_int, kern.reshape(1, KCOUNT), dist.T, nbr.T,
        send_index.reshape(2, GHOSTS), counts, cot, w_msg, w_rad, w_q, w_o,
    )
    return pl.pallas_call(
        finish,
        out_shape=shapes,
        in_specs=[hbm] * 5,
        out_specs=(hbm,) * 5,
        scratch_shapes=[buf(*t.shape, dtype=F32) for t in shapes] + [pltpu.SemaphoreType.DMA((10,))],
        compiler_params=pltpu.CompilerParams(vmem_limit_bytes=VMEM_BYTES),
        name="finish",
    )(*sums)


def solution(mesh):
    rows = P(("dom", "sub"), None)
    placed = (
        rows, P(None, ("dom", "sub")), P(), P(), rows, rows,
        P(("dom", "sub"), None, None), P(("dom", "sub")), rows, P(), P(), P(), P(),
    )
    return jax.shard_map(
        on_device,
        mesh=mesh,
        in_specs=placed,
        out_specs=(rows, P(), P(), P(), P()),
        check_vma=False,
    )
```

```python
import math

import jax
import jax.numpy as jnp
import numpy as np
from jax import lax
from jax.experimental import pallas as pl
from jax.experimental.pallas import tpu as pltpu
from jax.sharding import PartitionSpec as P

MESH = pl.DeviceIdType.MESH
BF = jnp.bfloat16
F32 = jnp.float32

WIDTH, GHOSTS, CHANS, SLOTS, KCOUNT, NB = 512, 128, 128, 64, 1024, 16
BLOCK, WINDOW = 128, 256
X, YZ, CORES = 4, 16, 2
CHIPS = X * YZ
PIECE = KCOUNT // CHIPS
QUART = KCOUNT // X
TOTAL = WIDTH * CHIPS * CORES
BOTH = 2 * CHANS
ROWS_AR = 24
VMEM_BYTES = 63 * 1024 * 1024


def fitted(fn, degree):
    nodes = (np.cos(np.pi * (np.arange(64) + 0.5) / 64) + 1.0) / 8.0
    series = np.polynomial.chebyshev.Chebyshev.fit(nodes, fn(nodes), degree, domain=[0.0, 0.25])
    return [float(np.float32(c)) for c in series.convert(kind=np.polynomial.Polynomial).coef]


COS = fitted(lambda y: np.cos(2 * np.pi * np.sqrt(y)), 6)
SIN = fitted(lambda y: np.sin(2 * np.pi * np.sqrt(y)) / np.sqrt(y), 5)


def horner(coefs, y):
    value = coefs[-1] * y + coefs[-2]
    for c in coefs[-3::-1]:
        value = value * y + c
    return value


def tn(a, b):
    return lax.dot_general(a, b, (((0,), (0,)), ((), ())), preferred_element_type=F32)


def nt(a, b):
    return lax.dot_general(a, b, (((1,), (1,)), ((), ())), preferred_element_type=F32)


def nn(a, b):
    return jnp.dot(a, b, preferred_element_type=F32)


def transposed(a):
    return jnp.transpose(a.astype(F32)).astype(a.dtype)


def kernel(
    feat_h, frac_h, kint_h, kern_h, dist_h, nbr_h, send_h, counts_h, cot_h, wmsg_h, wrad_h, wq_h, wo_h,
    gf_out, gmsg_out, rad_out, gwq_out, gwo_out,
    feat, frac, kint, kern, dist, nbr, send, counts, cot, wmsg, wrad, wq, wo,
    gf, gmsg_s, rad_s, gwq, gwo,
    table, sg_b, rc, xs, xs_b, rx, ag,
    fg, place_t, out_b, ghost, u_own, u_ghost,
    split_k, split_f, dz, env, lo_s, code_s, own_w, gmat, amat, ymat, gul, gug, radacc, gh_b, back, p_t, m_s,
    ar, ar1, ar2, fin, in_sem, out_sem, send_sem, recv_sem, rs_send, rs_recv, ag_send, ag_recv,
):
    pairs = [
        (kint_h, kint), (frac_h, frac), (counts_h, counts), (feat_h, feat), (cot_h, cot), (send_h, send),
        (dist_h, dist), (nbr_h, nbr), (wmsg_h, wmsg), (wrad_h, wrad), (kern_h, kern), (wq_h, wq), (wo_h, wo),
    ]
    loads = [pltpu.make_async_copy(src, dst, in_sem.at[i]) for i, (src, dst) in enumerate(pairs)]
    for c in loads:
        c.start()

    dom, sub = lax.axis_index("dom"), lax.axis_index("sub")
    x, zlo, y = dom // 8, (dom // 4) % 2, dom % 4
    zhi, core = sub // 2, sub % 2
    z = zhi * 2 + zlo
    yz = y * 4 + z
    chip = x * YZ + yz
    flat = dom * 4 + sub

    px = [(x + d) % 4 for d in range(4)]
    py = [(y + d) % 4 for d in range(4)]
    pz = [(z + d) % 4 for d in range(4)]
    far = [p * 8 for p in px]
    along = [(p % 2) * 4 for p in pz]
    pair_of = [(p // 2) * 2 for p in pz]
    both_cores = [core, 1 - core]

    def shifted(dx, dy, dz_, dc=0):
        where = (far[dx] + (along[dz_] + py[dy]), pair_of[dz_] + both_cores[dc])
        return px[dx] * YZ + (py[dy] * 4 + pz[dz_]), where

    def hops(turn):
        return sum(min(d, 4 - d) for d in turn)

    steps = (2, 1, 3, 0)
    turns = [(a, b, c) for a in range(4) for b in range(4) for c in range(4) if a or b or c]
    turns = sorted(turns, key=lambda t: (steps.index(t[0]), -hops(t)))
    places = [shifted(*t) for t in turns]
    plane = [(t, p) for t, p in zip(turns, places) if not t[0]]
    across = [(dx, dc) for dx in (2, 1, 3, 0) for dc in (1, 0) if dx or dc]
    across = [shifted(dx, 0, 0, dc)[1] for dx, dc in across]

    def group_of(dx):
        return [i for i, t in enumerate(turns) if t[0] == dx]

    other_core = (dom, zhi * 2 + 1 - core)
    upper, lower = (flat + 1) % 128, (flat + 127) % 128
    upper, lower = (upper // 4, upper % 4), (lower // 4, lower % 4)
    across = [(dx, dc) for dx in (2, 1, 3, 0) for dc in (1, 0) if dx or dc]
    across = [shifted(dx, 0, 0, dc)[1] for dx, dc in across]

    barrier = pltpu.get_barrier_semaphore()

    def greet(peer):
        pl.semaphore_signal(barrier, inc=1, device_id=peer, device_id_type=MESH)

    for _, peer in places:
        greet(peer)
    for peer in (upper, lower, other_core):
        greet(peer)
    for dx in range(1, X):
        greet(shifted(dx, 0, 0, 1)[1])
    greeted = CHIPS - 1 + 3 + X - 1

    sems = iter(range(48))

    def copy(src, dst, peer):
        at = next(sems)
        return pltpu.make_async_remote_copy(
            src_ref=src, dst_ref=dst, send_sem=send_sem.at[at], recv_sem=recv_sem.at[at],
            device_id=peer, device_id_type=MESH,
        )

    loads[0].wait()
    loads[1].wait()
    part = frac[...]
    blank = jnp.zeros((5, WIDTH), F32)
    pieces = []
    for _ in range(3):
        high = part.astype(BF).astype(F32)
        pieces += [high, blank]
        part = part - high
    split_f[...] = jnp.concatenate(pieces + [jnp.zeros((8, WIDTH), F32)], axis=0).astype(BF)
    k_rows = jnp.concatenate([kint[...].astype(F32), jnp.zeros((5, KCOUNT), F32)], axis=0)
    split_k[...] = jnp.concatenate([k_rows] * 3 + [jnp.zeros((8, KCOUNT), F32)], axis=0).astype(BF)

    def table_rows(step, _):
        base = pl.multiple_of(step * 256, 256)
        ks = split_k[:, pl.ds(base, 256)]
        for block in range(4):
            cols = slice(block * 128, block * 128 + 128)
            turns = tn(ks, split_f[:, cols])
            turns = turns - jnp.floor(turns + 0.5)
            square = turns * turns
            table[pl.ds(base, 256), cols] = horner(COS, square).astype(BF)
            table[pl.ds(KCOUNT + base, 256), cols] = (horner(SIN, square) * turns).astype(BF)
        return 0

    lax.fori_loop(0, KCOUNT // 256, table_rows, 0)

    for c in loads[2:5]:
        c.wait()
    live = lax.broadcasted_iota(jnp.int32, (WIDTH, CHANS), 0) < counts[0]
    fg[:, :CHANS] = jnp.where(live, feat[...].astype(F32), 0.0).astype(BF)
    fg[:, CHANS:] = jnp.where(live, cot[...].astype(F32), 0.0).astype(BF)
    theirs = pl.multiple_of((1 - core) * KCOUNT, KCOUNT)
    mine = pl.multiple_of(core * KCOUNT, KCOUNT)
    sg_b[...] = nn(table[pl.ds(theirs, KCOUNT), :], fg[...]).astype(BF)
    xs[...] = nn(table[pl.ds(mine, KCOUNT), :], fg[...])

    loads[5].wait()
    picks = jnp.concatenate([send[0:1, :], send[1:2, :]], axis=1)
    place_t[...] = jnp.where(
        lax.broadcasted_iota(jnp.int32, (WIDTH, 2 * GHOSTS), 0) == picks, 1.0, 0.0
    ).astype(BF)
    out_b[...] = tn(place_t[...], feat[...]).astype(BF)

    pl.semaphore_wait(barrier, greeted)

    halo = [
        copy(out_b.at[pl.ds(0, GHOSTS)], ghost.at[pl.ds(GHOSTS, GHOSTS)], lower),
        copy(out_b.at[pl.ds(GHOSTS, GHOSTS)], ghost.at[pl.ds(0, GHOSTS)], upper),
    ]
    quarters = [pl.ds(pl.multiple_of(px[dx] * QUART, QUART), QUART) for dx in range(4)]
    cores = [copy(sg_b.at[quarters[dx]], rc.at[quarters[dx]], other_core) for dx in steps]
    for c in cores[:2] + halo + cores[2:]:
        c.start()
    scatters = [
        pltpu.make_async_remote_copy(
            src_ref=xs_b.at[pl.ds(pl.multiple_of(to * PIECE, PIECE), PIECE)], dst_ref=rx.at[i],
            send_sem=rs_send.at[i], recv_sem=rs_recv.at[i], device_id=peer, device_id_type=MESH,
        )
        for i, (to, peer) in enumerate(places)
    ]
    for c in loads[6:]:
        c.wait()

    def spread_setup(pair):
        d_parts, p_parts = [], []
        for i in range(2):
            blk = 2 * pair + i
            w = min(max(blk * BLOCK - BLOCK // 2, 0), WIDTH - WINDOW)
            cols = slice(blk * BLOCK, (blk + 1) * BLOCK)
            n = nbr[:, cols]
            d_parts.append(dist[:, cols])
            place = jnp.where(n >= WIDTH, n - (WIDTH - WINDOW), n - w) + i * 2 * WINDOW
            p_parts.append(place.astype(F32))
        d2 = jnp.transpose(jnp.concatenate(d_parts, axis=0))
        place = jnp.concatenate(p_parts, axis=0)
        code = jnp.floor(place * (1.0 / 128.0))
        dz[pair] = d2 * (1.0 / 0.4)
        env[pair] = jnp.square(jnp.maximum(0.0, 1.0 - d2 * (1.0 / 6.0)))
        lo_s[pair] = place - code * 128.0
        code_s[pair] = jnp.transpose(code)

    def spread_blocks(pair):
        many = 64

        def group(step, _):
            base = pl.multiple_of(step * many, many)
            rows = pl.ds(base, many)
            dz_r, env_r, code_r = dz[pair, rows, :], env[pair, rows, :], code_s[pair, rows, :]
            lo_c = pltpu.roll(lo_s[pair], lax.rem(BLOCK - base, BLOCK), 1)
            b_ids = lax.broadcasted_iota(jnp.int32, (NB, 128), 0).astype(F32)
            lane = lax.broadcasted_iota(jnp.int32, (128, 128), 1).astype(F32).astype(BF)
            one, zero = jnp.ones((128, 128), BF), jnp.zeros((128, 128), BF)
            for s in range(many):
                gap = dz_r[s : s + 1, :] - b_ids
                basis = (jnp.exp(-(gap * gap)) * env_r[s : s + 1, :]).astype(BF)
                code = jnp.broadcast_to(code_r[s : s + 1, :], (NB, 128)).astype(BF)
                lhs = jnp.concatenate(
                    [jnp.where(code == h, basis, jnp.zeros_like(basis)) for h in range(8)], axis=0
                )
                low = jnp.broadcast_to(lo_c[:, s : s + 1], (128, 128)).astype(BF)
                out = nn(lhs, jnp.where(lane == low, one, zero)).astype(BF)
                for i in range(2):
                    at = pl.multiple_of(((2 * pair + i) * BLOCK + s) * NB + base * NB, NB)
                    for h in range(4):
                        r = (i * 4 + h) * NB
                        gmat[pl.ds(at, NB), h * 128 : h * 128 + 128] = out[r : r + NB, :]
            return 0

        lax.fori_loop(0, BLOCK // many, group, 0)

    spread_setup(0)
    spread_setup(1)

    weights = kern[...] * (1.0 / math.sqrt(KCOUNT * TOTAL))
    weights = pltpu.roll(weights, lax.rem(KCOUNT - chip * PIECE, KCOUNT), 1)[:, :CHANS]
    own_w[...] = jnp.transpose(jnp.broadcast_to(weights, (CHANS, CHANS)))[:PIECE, :]

    for dx, c in zip(steps, cores):
        c.wait()
        val = xs[quarters[dx], :] + rc[quarters[dx], :].astype(F32)
        xs_b[quarters[dx], :] = val.astype(BF)
        if not dx:
            xs[quarters[dx], :] = val
        for i in group_of(dx):
            scatters[i].start()

    spread_blocks(0)
    spread_blocks(1)

    u_own[...] = nn(feat[...], wmsg[...]).astype(BF)
    gul[...] = jnp.zeros_like(gul)
    gug[...] = jnp.zeros_like(gug)
    radacc[...] = jnp.zeros_like(radacc)
    wr = wrad[...].astype(F32)

    def window_of(blk):
        return pl.ds(min(max(blk * BLOCK - BLOCK // 2, 0), WIDTH - WINDOW), WINDOW)

    def rows_of(blk):
        return pl.ds(blk * BLOCK * NB, BLOCK * NB)

    blocks = WIDTH // BLOCK
    for blk in range(blocks):
        amat[rows_of(blk), :] = nn(gmat[rows_of(blk), :WINDOW], u_own[window_of(blk), :])
    for c in halo:
        c.wait()
    u_ghost[...] = nn(ghost[...], wmsg[...]).astype(BF)

    def gathered(blk):
        amat[rows_of(blk), :] += nn(gmat[rows_of(blk), WINDOW:], u_ghost[...])

    def atoms(blk):
        piece = 32
        for step in range(BLOCK // piece):
            at = blk * BLOCK + step * piece
            rows = pl.ds(at * NB, piece * NB)
            summed = amat[rows, :].reshape(piece, NB, CHANS)
            pre = jnp.sum(summed * wr[None], axis=1)
            sig = 1.0 / (1.0 + jnp.exp(-pre))
            gpre = fg[pl.ds(at, piece), CHANS:].astype(F32) * sig * (1.0 + pre * (1.0 - sig))
            wide = gpre[:, None, :]
            radacc[...] += jnp.sum(wide * summed, axis=0)
            ymat[rows, :] = (wide * wr[None]).reshape(piece * NB, CHANS).astype(BF)

    def scattered(blk):
        collected = jnp.transpose(tn(ymat[rows_of(blk), :], gmat[rows_of(blk), :]))
        gul[window_of(blk), :] += collected[:WINDOW, :]
        gug[...] += collected[WINDOW:, :]

    gathered(0)
    for blk in range(blocks):
        if blk + 1 < blocks:
            gathered(blk + 1)
        atoms(blk)
        if blk:
            scattered(blk - 1)
    scattered(blocks - 1)

    gu_g = gug[...].astype(BF)
    gu_l = gul[...].astype(BF)
    gmsg = tn(feat[...], gu_l) + tn(ghost[...], gu_g)

    ar[:, 0:16, :] = gmsg.reshape(8, 16, CHANS)
    ar[:, 16:24, :] = jnp.zeros((8, 8, CHANS), F32)
    for j in range(8):
        ar[j, 16:18, :] = radacc[2 * j : 2 * j + 2, :]
    me = x * 2 + core
    ar_first = []
    for o, peer in enumerate(across):
        ar_first.append(copy(ar.at[lax.rem(peer[0], 32) // 8 * 2 + lax.rem(peer[1], 2)], ar1.at[o], peer))
    for c in ar_first:
        c.start()

    gh_b[...] = nt(gu_g, wmsg[...]).astype(BF)
    returns = [
        copy(gh_b.at[pl.ds(0, GHOSTS)], back.at[pl.ds(GHOSTS, GHOSTS)], lower),
        copy(gh_b.at[pl.ds(GHOSTS, GHOSTS)], back.at[pl.ds(0, GHOSTS)], upper),
    ]
    for c in returns:
        c.start()

    gul[...] = fg[:, CHANS:].astype(F32) + nt(gu_l, wmsg[...])

    for c in scatters:
        c.wait()
    own = xs[pl.ds(pl.multiple_of(chip * PIECE, PIECE), PIECE), :]
    own = lax.fori_loop(0, CHIPS - 1, lambda i, v: v + rx[i].astype(F32), own)
    at_piece = pl.ds(pl.multiple_of(mine + chip * PIECE, PIECE), PIECE)
    ag[at_piece, :CHANS] = own[:, :CHANS].astype(BF)
    ag[at_piece, CHANS:] = (own[:, CHANS:] * own_w[...]).astype(BF)
    gathers = [
        pltpu.make_async_remote_copy(
            src_ref=ag.at[at_piece], dst_ref=ag.at[at_piece],
            send_sem=ag_send.at[i], recv_sem=ag_recv.at[i], device_id=peer, device_id_type=MESH,
        )
        for i, (_, peer) in enumerate(places)
    ]
    for c in gathers:
        c.start()


    for c in ar_first:
        c.wait()
    val = ar[me]
    for o in range(7):
        val = val + ar1[o]
    ar2[yz] = val
    ar_yz = [copy(ar2.at[yz], ar2.at[yz], peer) for _, (_, peer) in plane]
    for c in ar_yz:
        c.start()

    for c in ar_yz:
        c.wait()
    val = ar2[0]
    for j in range(1, YZ):
        val = val + ar2[j]
    fin[me] = val
    ar_fin = [copy(fin.at[me], fin.at[me], peer) for peer in across]
    for c in ar_fin:
        c.start()
    passed = []
    for dx in steps:
        for i in group_of(dx):
            gathers[i].wait()
        rows = pl.ds(pl.multiple_of(mine + px[(4 - dx) % 4] * QUART, QUART), QUART)
        passed.append(copy(ag.at[rows], ag.at[rows], other_core))
        passed[-1].start()

    def half_of(start, which):
        rows = pl.ds(start, KCOUNT)
        weighted = ag[rows, CHANS:]
        m_s[which] = tn(weighted, ag[rows, :CHANS])
        return tn(weighted, table[rows, :])

    p_t[...] = half_of(mine, core)
    for c in passed:
        c.wait()
    p_b = (p_t[...] + half_of(theirs, 1 - core)).astype(BF)
    gq_t = nn(wo[...], p_b).astype(BF)
    ghq = jnp.transpose(nn(wq[...], gq_t))
    base_grad = gul[...] + jnp.where(live, ghq, 0.0)
    for c in returns:
        c.wait()
    gf[...] = base_grad + nn(place_t[...], back[...])
    outs = [
        pltpu.make_async_copy(src, dst, out_sem.at[i])
        for i, (src, dst) in enumerate(
            [(gf, gf_out), (gwq, gwq_out), (gwo, gwo_out), (gmsg_s, gmsg_out), (rad_s, rad_out)]
        )
    ]
    outs[0].start()

    rscale = 1.0 / math.sqrt(TOTAL)
    m_full = jnp.transpose(m_s[0] + m_s[1])
    m_hi = m_full.astype(BF)
    m_lo = (m_full - m_hi.astype(F32)).astype(BF)
    gwq[...] = (nt(m_hi, wo[...]) + nt(m_lo, wo[...])) * rscale
    wq_t = transposed(wq[...])
    gwo[...] = (nn(wq_t, m_hi) + nn(wq_t, m_lo)) * rscale
    outs[1].start()
    outs[2].start()

    for c in ar_fin:
        c.wait()
    gmsg_s[...] = fin[:, 0:16, :].reshape(CHANS, CHANS) * rscale
    outs[3].start()
    for j in range(8):
        rad_s[2 * j : 2 * j + 2, :] = fin[j, 16:18, :] * (rscale / math.sqrt(SLOTS))
    outs[4].start()
    for c in outs:
        c.wait()


def finish(*refs):
    ins, outs, held, sem = refs[:5], refs[5:10], refs[10:15], refs[15]
    reads = [pltpu.make_async_copy(ins[i], held[i], sem.at[i]) for i in range(5)]
    writes = [pltpu.make_async_copy(held[i], outs[i], sem.at[5 + i]) for i in range(5)]
    for r in reads:
        r.start()
    for r, w in zip(reads, writes):
        r.wait()
        w.start()
    for w in writes:
        w.wait()


def on_device(features, frac, k_int, kern, dist, nbr, send_index, counts, cot, w_msg, w_rad, w_q, w_o):
    hbm = pl.BlockSpec(memory_space=pltpu.HBM)

    def buf(*shape, dtype=BF):
        return pltpu.VMEM(shape, dtype)

    def result(*shape):
        return jax.ShapeDtypeStruct(shape, F32)

    shapes = (result(WIDTH, CHANS), result(CHANS, CHANS), result(NB, CHANS), result(CHANS, CHANS), result(CHANS, CHANS))
    sums = pl.pallas_call(
        kernel,
        out_shape=shapes,
        in_specs=[hbm] * 13,
        out_specs=(hbm,) * 5,
        scratch_shapes=[
            buf(WIDTH, CHANS),
            buf(3, WIDTH, dtype=F32),
            buf(3, KCOUNT, dtype=jnp.int32),
            buf(1, KCOUNT, dtype=F32),
            buf(SLOTS, WIDTH, dtype=F32),
            buf(SLOTS, WIDTH, dtype=jnp.int32),
            buf(2, GHOSTS, dtype=jnp.int32),
            pltpu.SMEM((1,), jnp.int32),
            buf(WIDTH, CHANS),
            buf(CHANS, CHANS),
            buf(NB, CHANS),
            buf(CHANS, CHANS),
            buf(CHANS, CHANS),
            buf(WIDTH, CHANS, dtype=F32),
            buf(CHANS, CHANS, dtype=F32),
            buf(NB, CHANS, dtype=F32),
            buf(CHANS, CHANS, dtype=F32),
            buf(CHANS, CHANS, dtype=F32),
            buf(2 * KCOUNT, WIDTH),
            buf(KCOUNT, BOTH),
            buf(KCOUNT, BOTH),
            buf(KCOUNT, BOTH, dtype=F32),
            buf(KCOUNT, BOTH),
            buf(CHIPS - 1, PIECE, BOTH),
            buf(2 * KCOUNT, BOTH),
            buf(WIDTH, BOTH),
            buf(WIDTH, 2 * GHOSTS),
            buf(2 * GHOSTS, CHANS),
            buf(2 * GHOSTS, CHANS),
            buf(WIDTH, CHANS),
            buf(2 * GHOSTS, CHANS),
            buf(32, KCOUNT),
            buf(32, WIDTH),
            buf(2, BLOCK, 128, dtype=F32),
            buf(2, BLOCK, 128, dtype=F32),
            buf(2, BLOCK, 128, dtype=F32),
            buf(2, BLOCK, 128, dtype=F32),
            buf(PIECE, CHANS, dtype=F32),
            buf(WIDTH * NB, 2 * WINDOW),
            buf(WIDTH * NB, CHANS, dtype=F32),
            buf(WIDTH * NB, CHANS),
            buf(WIDTH, CHANS, dtype=F32),
            buf(2 * GHOSTS, CHANS, dtype=F32),
            buf(NB, CHANS, dtype=F32),
            buf(2 * GHOSTS, CHANS),
            buf(2 * GHOSTS, CHANS),
            buf(CHANS, WIDTH, dtype=F32),
            buf(2, CHANS, CHANS, dtype=F32),
            buf(8, ROWS_AR, CHANS, dtype=F32),
            buf(7, ROWS_AR, CHANS, dtype=F32),
            buf(YZ, ROWS_AR, CHANS, dtype=F32),
            buf(8, ROWS_AR, CHANS, dtype=F32),
            pltpu.SemaphoreType.DMA((13,)),
            pltpu.SemaphoreType.DMA((5,)),
            pltpu.SemaphoreType.DMA((48,)),
            pltpu.SemaphoreType.DMA((48,)),
            pltpu.SemaphoreType.DMA((CHIPS - 1,)),
            pltpu.SemaphoreType.DMA((CHIPS - 1,)),
            pltpu.SemaphoreType.DMA((CHIPS - 1,)),
            pltpu.SemaphoreType.DMA((CHIPS - 1,)),
        ],
        compiler_params=pltpu.CompilerParams(
            collective_id=0, has_side_effects=True, vmem_limit_bytes=VMEM_BYTES
        ),
        name="ewald_backward",
    )(
        features, frac, k_int, kern.reshape(1, KCOUNT), dist.T, nbr.T,
        send_index.reshape(2, GHOSTS), counts, cot, w_msg, w_rad, w_q, w_o,
    )
    return pl.pallas_call(
        finish,
        out_shape=shapes,
        in_specs=[hbm] * 5,
        out_specs=(hbm,) * 5,
        scratch_shapes=[buf(*t.shape, dtype=F32) for t in shapes] + [pltpu.SemaphoreType.DMA((10,))],
        compiler_params=pltpu.CompilerParams(vmem_limit_bytes=VMEM_BYTES),
        name="finish",
    )(*sums)


def solution(mesh):
    rows = P(("dom", "sub"), None)
    placed = (
        rows, P(None, ("dom", "sub")), P(), P(), rows, rows,
        P(("dom", "sub"), None, None), P(("dom", "sub")), rows, P(), P(), P(), P(),
    )
    return jax.shard_map(
        on_device,
        mesh=mesh,
        in_specs=placed,
        out_specs=(rows, P(), P(), P(), P()),
        check_vma=False,
    )
```

```python
import math

import jax
import jax.numpy as jnp
import numpy as np
from jax import lax
from jax.experimental import pallas as pl
from jax.experimental.pallas import tpu as pltpu
from jax.sharding import PartitionSpec as P

MESH = pl.DeviceIdType.MESH
BF = jnp.bfloat16
F32 = jnp.float32

WIDTH, GHOSTS, CHANS, SLOTS, KCOUNT, NB = 512, 128, 128, 64, 1024, 16
BLOCK, WINDOW = 128, 256
X, YZ, CORES = 4, 16, 2
CHIPS = X * YZ
PIECE = KCOUNT // CHIPS
QUART = KCOUNT // X
TOTAL = WIDTH * CHIPS * CORES
BOTH = 2 * CHANS
ROWS_AR = 24
VMEM_BYTES = 63 * 1024 * 1024


def fitted(fn, degree):
    nodes = (np.cos(np.pi * (np.arange(64) + 0.5) / 64) + 1.0) / 8.0
    series = np.polynomial.chebyshev.Chebyshev.fit(nodes, fn(nodes), degree, domain=[0.0, 0.25])
    return [float(np.float32(c)) for c in series.convert(kind=np.polynomial.Polynomial).coef]


COS = fitted(lambda y: np.cos(2 * np.pi * np.sqrt(y)), 5)
SIN = fitted(lambda y: np.sin(2 * np.pi * np.sqrt(y)) / np.sqrt(y), 5)


def horner(coefs, y):
    value = coefs[-1] * y + coefs[-2]
    for c in coefs[-3::-1]:
        value = value * y + c
    return value


def tn(a, b):
    return lax.dot_general(a, b, (((0,), (0,)), ((), ())), preferred_element_type=F32)


def nt(a, b):
    return lax.dot_general(a, b, (((1,), (1,)), ((), ())), preferred_element_type=F32)


def nn(a, b):
    return jnp.dot(a, b, preferred_element_type=F32)


def transposed(a):
    return jnp.transpose(a.astype(F32)).astype(a.dtype)


def kernel(
    feat_h, frac_h, kint_h, kern_h, dist_h, nbr_h, send_h, counts_h, cot_h, wmsg_h, wrad_h, wq_h, wo_h,
    gf_out, gmsg_out, rad_out, gwq_out, gwo_out,
    feat, frac, kint, kern, dist, nbr, send, counts, cot, wmsg, wrad, wq, wo,
    gf, gmsg_s, rad_s, gwq, gwo,
    table, sg_b, rc, xs, xs_b, rx, ag,
    fg, place_t, out_b, ghost, u_own, u_ghost,
    split_k, split_f, dz, env, lo_s, code_s, own_w, gmat, amat, ymat, gul, gug, radacc, gh_b, back, p_t, m_s,
    ar, ar1, ar2, fin, in_sem, out_sem, send_sem, recv_sem, rs_send, rs_recv, ag_send, ag_recv,
):
    pairs = [
        (kint_h, kint), (frac_h, frac), (counts_h, counts), (feat_h, feat), (cot_h, cot), (send_h, send),
        (dist_h, dist), (nbr_h, nbr), (wmsg_h, wmsg), (wrad_h, wrad), (kern_h, kern), (wq_h, wq), (wo_h, wo),
    ]
    loads = [pltpu.make_async_copy(src, dst, in_sem.at[i]) for i, (src, dst) in enumerate(pairs)]
    for c in loads:
        c.start()

    dom, sub = lax.axis_index("dom"), lax.axis_index("sub")
    x, zlo, y = dom // 8, (dom // 4) % 2, dom % 4
    zhi, core = sub // 2, sub % 2
    z = zhi * 2 + zlo
    yz = y * 4 + z
    chip = x * YZ + yz
    flat = dom * 4 + sub

    px = [(x + d) % 4 for d in range(4)]
    py = [(y + d) % 4 for d in range(4)]
    pz = [(z + d) % 4 for d in range(4)]
    far = [p * 8 for p in px]
    along = [(p % 2) * 4 for p in pz]
    pair_of = [(p // 2) * 2 for p in pz]
    both_cores = [core, 1 - core]

    def shifted(dx, dy, dz_, dc=0):
        where = (far[dx] + (along[dz_] + py[dy]), pair_of[dz_] + both_cores[dc])
        return px[dx] * YZ + (py[dy] * 4 + pz[dz_]), where

    def hops(turn):
        return sum(min(d, 4 - d) for d in turn)

    steps = (2, 1, 3, 0)
    turns = [(a, b, c) for a in range(4) for b in range(4) for c in range(4) if a or b or c]
    turns = sorted(turns, key=lambda t: (steps.index(t[0]), -hops(t)))
    places = [shifted(*t) for t in turns]
    plane = [(t, p) for t, p in zip(turns, places) if not t[0]]
    across = [(dx, dc) for dx in (2, 1, 3, 0) for dc in (1, 0) if dx or dc]
    across = [shifted(dx, 0, 0, dc)[1] for dx, dc in across]

    def group_of(dx):
        return [i for i, t in enumerate(turns) if t[0] == dx]

    other_core = (dom, zhi * 2 + 1 - core)
    upper, lower = (flat + 1) % 128, (flat + 127) % 128
    upper, lower = (upper // 4, upper % 4), (lower // 4, lower % 4)
    across = [(dx, dc) for dx in (2, 1, 3, 0) for dc in (1, 0) if dx or dc]
    across = [shifted(dx, 0, 0, dc)[1] for dx, dc in across]

    barrier = pltpu.get_barrier_semaphore()

    def greet(peer):
        pl.semaphore_signal(barrier, inc=1, device_id=peer, device_id_type=MESH)

    for _, peer in places:
        greet(peer)
    for peer in (upper, lower, other_core):
        greet(peer)
    for dx in range(1, X):
        greet(shifted(dx, 0, 0, 1)[1])
    greeted = CHIPS - 1 + 3 + X - 1

    sems = iter(range(48))

    def copy(src, dst, peer):
        at = next(sems)
        return pltpu.make_async_remote_copy(
            src_ref=src, dst_ref=dst, send_sem=send_sem.at[at], recv_sem=recv_sem.at[at],
            device_id=peer, device_id_type=MESH,
        )

    loads[0].wait()
    loads[1].wait()
    part = frac[...]
    blank = jnp.zeros((5, WIDTH), F32)
    pieces = []
    for _ in range(3):
        high = part.astype(BF).astype(F32)
        pieces += [high, blank]
        part = part - high
    split_f[...] = jnp.concatenate(pieces + [jnp.zeros((8, WIDTH), F32)], axis=0).astype(BF)
    k_rows = jnp.concatenate([kint[...].astype(F32), jnp.zeros((5, KCOUNT), F32)], axis=0)
    split_k[...] = jnp.concatenate([k_rows] * 3 + [jnp.zeros((8, KCOUNT), F32)], axis=0).astype(BF)

    def table_rows(step, _):
        base = pl.multiple_of(step * 256, 256)
        ks = split_k[:, pl.ds(base, 256)]
        for block in range(4):
            cols = slice(block * 128, block * 128 + 128)
            turns = tn(ks, split_f[:, cols])
            turns = turns - jnp.floor(turns + 0.5)
            square = turns * turns
            table[pl.ds(base, 256), cols] = horner(COS, square).astype(BF)
            table[pl.ds(KCOUNT + base, 256), cols] = (horner(SIN, square) * turns).astype(BF)
        return 0

    lax.fori_loop(0, KCOUNT // 256, table_rows, 0)

    for c in loads[2:5]:
        c.wait()
    live = lax.broadcasted_iota(jnp.int32, (WIDTH, CHANS), 0) < counts[0]
    fg[:, :CHANS] = jnp.where(live, feat[...].astype(F32), 0.0).astype(BF)
    fg[:, CHANS:] = jnp.where(live, cot[...].astype(F32), 0.0).astype(BF)
    theirs = pl.multiple_of((1 - core) * KCOUNT, KCOUNT)
    mine = pl.multiple_of(core * KCOUNT, KCOUNT)
    sg_b[...] = nn(table[pl.ds(theirs, KCOUNT), :], fg[...]).astype(BF)
    xs[...] = nn(table[pl.ds(mine, KCOUNT), :], fg[...])

    loads[5].wait()
    picks = jnp.concatenate([send[0:1, :], send[1:2, :]], axis=1)
    place_t[...] = jnp.where(
        lax.broadcasted_iota(jnp.int32, (WIDTH, 2 * GHOSTS), 0) == picks, 1.0, 0.0
    ).astype(BF)
    out_b[...] = tn(place_t[...], feat[...]).astype(BF)

    pl.semaphore_wait(barrier, greeted)

    halo = [
        copy(out_b.at[pl.ds(0, GHOSTS)], ghost.at[pl.ds(GHOSTS, GHOSTS)], lower),
        copy(out_b.at[pl.ds(GHOSTS, GHOSTS)], ghost.at[pl.ds(0, GHOSTS)], upper),
    ]
    quarters = [pl.ds(pl.multiple_of(px[dx] * QUART, QUART), QUART) for dx in range(4)]
    cores = [copy(sg_b.at[quarters[dx]], rc.at[quarters[dx]], other_core) for dx in steps]
    for c in cores[:2] + halo + cores[2:]:
        c.start()
    scatters = [
        pltpu.make_async_remote_copy(
            src_ref=xs_b.at[pl.ds(pl.multiple_of(to * PIECE, PIECE), PIECE)], dst_ref=rx.at[i],
            send_sem=rs_send.at[i], recv_sem=rs_recv.at[i], device_id=peer, device_id_type=MESH,
        )
        for i, (to, peer) in enumerate(places)
    ]
    for c in loads[6:]:
        c.wait()

    def spread_setup(pair):
        d_parts, p_parts = [], []
        for i in range(2):
            blk = 2 * pair + i
            w = min(max(blk * BLOCK - BLOCK // 2, 0), WIDTH - WINDOW)
            cols = slice(blk * BLOCK, (blk + 1) * BLOCK)
            n = nbr[:, cols]
            d_parts.append(dist[:, cols])
            place = jnp.where(n >= WIDTH, n - (WIDTH - WINDOW), n - w) + i * 2 * WINDOW
            p_parts.append(place.astype(F32))
        d2 = jnp.transpose(jnp.concatenate(d_parts, axis=0))
        place = jnp.concatenate(p_parts, axis=0)
        code = jnp.floor(place * (1.0 / 128.0))
        dz[pair] = d2 * (1.0 / 0.4)
        env[pair] = jnp.square(jnp.maximum(0.0, 1.0 - d2 * (1.0 / 6.0)))
        lo_s[pair] = place - code * 128.0
        code_s[pair] = jnp.transpose(code)

    def spread_blocks(first, last):
        many = 64

        def group(step, _):
            pair = step // 2
            base = pl.multiple_of(step % 2 * many, many)
            rows = pl.ds(base, many)
            dz_r, env_r, code_r = dz[pair, rows, :], env[pair, rows, :], code_s[pair, rows, :]
            lo_c = pltpu.roll(lo_s[pair], lax.rem(BLOCK - base, BLOCK), 1)
            b_ids = lax.broadcasted_iota(jnp.int32, (NB, 128), 0).astype(F32)
            lane = lax.broadcasted_iota(jnp.int32, (128, 128), 1).astype(F32).astype(BF)
            one, zero = jnp.ones((128, 128), BF), jnp.zeros((128, 128), BF)
            for s in range(many):
                gap = dz_r[s : s + 1, :] - b_ids
                basis = (jnp.exp(-(gap * gap)) * env_r[s : s + 1, :]).astype(BF)
                code = jnp.broadcast_to(code_r[s : s + 1, :], (NB, 128)).astype(BF)
                lhs = jnp.concatenate(
                    [jnp.where(code == h, basis, jnp.zeros_like(basis)) for h in range(8)], axis=0
                )
                low = jnp.broadcast_to(lo_c[:, s : s + 1], (128, 128)).astype(BF)
                out = nn(lhs, jnp.where(lane == low, one, zero)).astype(BF)
                for i in range(2):
                    at = pl.multiple_of((2 * pair + i) * BLOCK * NB + base * NB + s * NB, NB)
                    for h in range(4):
                        r = (i * 4 + h) * NB
                        gmat[pl.ds(at, NB), h * 128 : h * 128 + 128] = out[r : r + NB, :]
            return 0

        lax.fori_loop(first, last, group, 0)

    spread_setup(0)
    spread_setup(1)

    weights = kern[...] * (1.0 / math.sqrt(KCOUNT * TOTAL))
    weights = pltpu.roll(weights, lax.rem(KCOUNT - chip * PIECE, KCOUNT), 1)[:, :CHANS]
    own_w[...] = jnp.transpose(jnp.broadcast_to(weights, (CHANS, CHANS)))[:PIECE, :]

    spread_blocks(0, 1)

    for dx, c in zip(steps, cores):
        c.wait()
        val = xs[quarters[dx], :] + rc[quarters[dx], :].astype(F32)
        xs_b[quarters[dx], :] = val.astype(BF)
        if not dx:
            xs[quarters[dx], :] = val
        for i in group_of(dx):
            scatters[i].start()

    spread_blocks(1, 4)

    u_own[...] = nn(feat[...], wmsg[...]).astype(BF)
    gul[...] = jnp.zeros_like(gul)
    gug[...] = jnp.zeros_like(gug)
    radacc[...] = jnp.zeros_like(radacc)
    wr = wrad[...].astype(F32)

    def window_of(blk):
        return pl.ds(min(max(blk * BLOCK - BLOCK // 2, 0), WIDTH - WINDOW), WINDOW)

    def rows_of(blk):
        return pl.ds(blk * BLOCK * NB, BLOCK * NB)

    blocks = WIDTH // BLOCK
    for blk in range(blocks):
        amat[rows_of(blk), :] = nn(gmat[rows_of(blk), :WINDOW], u_own[window_of(blk), :])
    for c in halo:
        c.wait()
    u_ghost[...] = nn(ghost[...], wmsg[...]).astype(BF)

    def gathered(blk):
        amat[rows_of(blk), :] += nn(gmat[rows_of(blk), WINDOW:], u_ghost[...])

    def atoms(blk):
        piece = 32
        for step in range(BLOCK // piece):
            at = blk * BLOCK + step * piece
            rows = pl.ds(at * NB, piece * NB)
            summed = amat[rows, :].reshape(piece, NB, CHANS)
            pre = jnp.sum(summed * wr[None], axis=1)
            sig = 1.0 / (1.0 + jnp.exp(-pre))
            gpre = fg[pl.ds(at, piece), CHANS:].astype(F32) * sig * (1.0 + pre * (1.0 - sig))
            wide = gpre[:, None, :]
            radacc[...] += jnp.sum(wide * summed, axis=0)
            ymat[rows, :] = (wide * wr[None]).reshape(piece * NB, CHANS).astype(BF)

    def scattered(blk):
        collected = jnp.transpose(tn(ymat[rows_of(blk), :], gmat[rows_of(blk), :]))
        gul[window_of(blk), :] += collected[:WINDOW, :]
        gug[...] += collected[WINDOW:, :]

    gathered(0)
    for blk in range(blocks):
        if blk + 1 < blocks:
            gathered(blk + 1)
        atoms(blk)
        if blk:
            scattered(blk - 1)
    scattered(blocks - 1)

    gu_g = gug[...].astype(BF)
    gu_l = gul[...].astype(BF)
    gmsg = tn(feat[...], gu_l) + tn(ghost[...], gu_g)

    ar[:, 0:16, :] = gmsg.reshape(8, 16, CHANS)
    ar[:, 16:24, :] = jnp.zeros((8, 8, CHANS), F32)
    for j in range(8):
        ar[j, 16:18, :] = radacc[2 * j : 2 * j + 2, :]
    me = x * 2 + core
    ar_first = []
    for o, peer in enumerate(across):
        ar_first.append(copy(ar.at[lax.rem(peer[0], 32) // 8 * 2 + lax.rem(peer[1], 2)], ar1.at[o], peer))
    for c in ar_first:
        c.start()

    gh_b[...] = nt(gu_g, wmsg[...]).astype(BF)
    returns = [
        copy(gh_b.at[pl.ds(0, GHOSTS)], back.at[pl.ds(GHOSTS, GHOSTS)], lower),
        copy(gh_b.at[pl.ds(GHOSTS, GHOSTS)], back.at[pl.ds(0, GHOSTS)], upper),
    ]
    for c in returns:
        c.start()

    gul[...] = fg[:, CHANS:].astype(F32) + nt(gu_l, wmsg[...])

    for c in scatters:
        c.wait()
    own = xs[pl.ds(pl.multiple_of(chip * PIECE, PIECE), PIECE), :]
    def add_some(step, total):
        for j in range(9):
            total = total + rx[step * 9 + j].astype(F32)
        return total

    own = lax.fori_loop(0, (CHIPS - 1) // 9, add_some, own)
    at_piece = pl.ds(pl.multiple_of(mine + chip * PIECE, PIECE), PIECE)
    ag[at_piece, :CHANS] = own[:, :CHANS].astype(BF)
    ag[at_piece, CHANS:] = (own[:, CHANS:] * own_w[...]).astype(BF)
    gathers = [
        pltpu.make_async_remote_copy(
            src_ref=ag.at[at_piece], dst_ref=ag.at[at_piece],
            send_sem=ag_send.at[i], recv_sem=ag_recv.at[i], device_id=peer, device_id_type=MESH,
        )
        for i, (_, peer) in enumerate(places)
    ]
    for c in gathers:
        c.start()


    for c in ar_first:
        c.wait()
    val = ar[me]
    for o in range(7):
        val = val + ar1[o]
    ar2[yz] = val
    ar_yz = [copy(ar2.at[yz], ar2.at[yz], peer) for _, (_, peer) in plane]
    for c in ar_yz:
        c.start()

    for c in ar_yz:
        c.wait()
    val = ar2[0]
    for j in range(1, YZ):
        val = val + ar2[j]
    fin[me] = val
    ar_fin = [copy(fin.at[me], fin.at[me], peer) for peer in across]
    for c in ar_fin:
        c.start()
    passed = []
    for dx in steps:
        for i in group_of(dx):
            gathers[i].wait()
        rows = pl.ds(pl.multiple_of(mine + px[(4 - dx) % 4] * QUART, QUART), QUART)
        passed.append(copy(ag.at[rows], ag.at[rows], other_core))
        passed[-1].start()

    def half_of(start, which):
        rows = pl.ds(start, KCOUNT)
        weighted = ag[rows, CHANS:]
        m_s[which] = tn(weighted, ag[rows, :CHANS])
        return tn(weighted, table[rows, :])

    p_t[...] = half_of(mine, core)
    for c in passed:
        c.wait()
    p_b = (p_t[...] + half_of(theirs, 1 - core)).astype(BF)
    gq_t = nn(wo[...], p_b).astype(BF)
    ghq = jnp.transpose(nn(wq[...], gq_t))
    base_grad = gul[...] + jnp.where(live, ghq, 0.0)
    for c in returns:
        c.wait()
    gf[...] = base_grad + nn(place_t[...], back[...])
    outs = [
        pltpu.make_async_copy(src, dst, out_sem.at[i])
        for i, (src, dst) in enumerate(
            [(gf, gf_out), (gwq, gwq_out), (gwo, gwo_out), (gmsg_s, gmsg_out), (rad_s, rad_out)]
        )
    ]
    outs[0].start()

    rscale = 1.0 / math.sqrt(TOTAL)
    m_full = jnp.transpose(m_s[0] + m_s[1])
    m_hi = m_full.astype(BF)
    m_lo = (m_full - m_hi.astype(F32)).astype(BF)
    gwq[...] = (nt(m_hi, wo[...]) + nt(m_lo, wo[...])) * rscale
    wq_t = transposed(wq[...])
    gwo[...] = (nn(wq_t, m_hi) + nn(wq_t, m_lo)) * rscale
    outs[1].start()
    outs[2].start()

    for c in ar_fin:
        c.wait()
    gmsg_s[...] = fin[:, 0:16, :].reshape(CHANS, CHANS) * rscale
    outs[3].start()
    for j in range(8):
        rad_s[2 * j : 2 * j + 2, :] = fin[j, 16:18, :] * (rscale / math.sqrt(SLOTS))
    outs[4].start()
    for c in outs:
        c.wait()


def finish(*refs):
    ins, outs, held, sem = refs[:5], refs[5:10], refs[10:15], refs[15]
    reads = [pltpu.make_async_copy(ins[i], held[i], sem.at[i]) for i in range(5)]
    writes = [pltpu.make_async_copy(held[i], outs[i], sem.at[5 + i]) for i in range(5)]
    for r in reads:
        r.start()
    for r, w in zip(reads, writes):
        r.wait()
        w.start()
    for w in writes:
        w.wait()


def on_device(features, frac, k_int, kern, dist, nbr, send_index, counts, cot, w_msg, w_rad, w_q, w_o):
    hbm = pl.BlockSpec(memory_space=pltpu.HBM)

    def buf(*shape, dtype=BF):
        return pltpu.VMEM(shape, dtype)

    def result(*shape):
        return jax.ShapeDtypeStruct(shape, F32)

    shapes = (result(WIDTH, CHANS), result(CHANS, CHANS), result(NB, CHANS), result(CHANS, CHANS), result(CHANS, CHANS))
    sums = pl.pallas_call(
        kernel,
        out_shape=shapes,
        in_specs=[hbm] * 13,
        out_specs=(hbm,) * 5,
        scratch_shapes=[
            buf(WIDTH, CHANS),
            buf(3, WIDTH, dtype=F32),
            buf(3, KCOUNT, dtype=jnp.int32),
            buf(1, KCOUNT, dtype=F32),
            buf(SLOTS, WIDTH, dtype=F32),
            buf(SLOTS, WIDTH, dtype=jnp.int32),
            buf(2, GHOSTS, dtype=jnp.int32),
            pltpu.SMEM((1,), jnp.int32),
            buf(WIDTH, CHANS),
            buf(CHANS, CHANS),
            buf(NB, CHANS),
            buf(CHANS, CHANS),
            buf(CHANS, CHANS),
            buf(WIDTH, CHANS, dtype=F32),
            buf(CHANS, CHANS, dtype=F32),
            buf(NB, CHANS, dtype=F32),
            buf(CHANS, CHANS, dtype=F32),
            buf(CHANS, CHANS, dtype=F32),
            buf(2 * KCOUNT, WIDTH),
            buf(KCOUNT, BOTH),
            buf(KCOUNT, BOTH),
            buf(KCOUNT, BOTH, dtype=F32),
            buf(KCOUNT, BOTH),
            buf(CHIPS - 1, PIECE, BOTH),
            buf(2 * KCOUNT, BOTH),
            buf(WIDTH, BOTH),
            buf(WIDTH, 2 * GHOSTS),
            buf(2 * GHOSTS, CHANS),
            buf(2 * GHOSTS, CHANS),
            buf(WIDTH, CHANS),
            buf(2 * GHOSTS, CHANS),
            buf(32, KCOUNT),
            buf(32, WIDTH),
            buf(2, BLOCK, 128, dtype=F32),
            buf(2, BLOCK, 128, dtype=F32),
            buf(2, BLOCK, 128, dtype=F32),
            buf(2, BLOCK, 128, dtype=F32),
            buf(PIECE, CHANS, dtype=F32),
            buf(WIDTH * NB, 2 * WINDOW),
            buf(WIDTH * NB, CHANS, dtype=F32),
            buf(WIDTH * NB, CHANS),
            buf(WIDTH, CHANS, dtype=F32),
            buf(2 * GHOSTS, CHANS, dtype=F32),
            buf(NB, CHANS, dtype=F32),
            buf(2 * GHOSTS, CHANS),
            buf(2 * GHOSTS, CHANS),
            buf(CHANS, WIDTH, dtype=F32),
            buf(2, CHANS, CHANS, dtype=F32),
            buf(8, ROWS_AR, CHANS, dtype=F32),
            buf(7, ROWS_AR, CHANS, dtype=F32),
            buf(YZ, ROWS_AR, CHANS, dtype=F32),
            buf(8, ROWS_AR, CHANS, dtype=F32),
            pltpu.SemaphoreType.DMA((13,)),
            pltpu.SemaphoreType.DMA((5,)),
            pltpu.SemaphoreType.DMA((48,)),
            pltpu.SemaphoreType.DMA((48,)),
            pltpu.SemaphoreType.DMA((CHIPS - 1,)),
            pltpu.SemaphoreType.DMA((CHIPS - 1,)),
            pltpu.SemaphoreType.DMA((CHIPS - 1,)),
            pltpu.SemaphoreType.DMA((CHIPS - 1,)),
        ],
        compiler_params=pltpu.CompilerParams(
            collective_id=0, has_side_effects=True, vmem_limit_bytes=VMEM_BYTES
        ),
        name="ewald_backward",
    )(
        features, frac, k_int, kern.reshape(1, KCOUNT), dist.T, nbr.T,
        send_index.reshape(2, GHOSTS), counts, cot, w_msg, w_rad, w_q, w_o,
    )
    return pl.pallas_call(
        finish,
        out_shape=shapes,
        in_specs=[hbm] * 5,
        out_specs=(hbm,) * 5,
        scratch_shapes=[buf(*t.shape, dtype=F32) for t in shapes] + [pltpu.SemaphoreType.DMA((10,))],
        compiler_params=pltpu.CompilerParams(vmem_limit_bytes=VMEM_BYTES),
        name="finish",
    )(*sums)


def solution(mesh):
    rows = P(("dom", "sub"), None)
    placed = (
        rows, P(None, ("dom", "sub")), P(), P(), rows, rows,
        P(("dom", "sub"), None, None), P(("dom", "sub")), rows, P(), P(), P(), P(),
    )
    return jax.shard_map(
        on_device,
        mesh=mesh,
        in_specs=placed,
        out_specs=(rows, P(), P(), P(), P()),
        check_vma=False,
    )
```

```python
import math

import jax
import jax.numpy as jnp
import numpy as np
from jax import lax
from jax.experimental import pallas as pl
from jax.experimental.pallas import tpu as pltpu
from jax.sharding import PartitionSpec as P

MESH = pl.DeviceIdType.MESH
BF = jnp.bfloat16
F32 = jnp.float32

WIDTH, GHOSTS, CHANS, SLOTS, KCOUNT, NB = 512, 128, 128, 64, 1024, 16
BLOCK, WINDOW = 128, 256
X, YZ, CORES = 4, 16, 2
CHIPS = X * YZ
PIECE = KCOUNT // CHIPS
QUART = KCOUNT // X
TOTAL = WIDTH * CHIPS * CORES
BOTH = 2 * CHANS
ROWS_AR = 24
VMEM_BYTES = 63 * 1024 * 1024


def fitted(fn, degree):
    nodes = (np.cos(np.pi * (np.arange(64) + 0.5) / 64) + 1.0) / 8.0
    series = np.polynomial.chebyshev.Chebyshev.fit(nodes, fn(nodes), degree, domain=[0.0, 0.25])
    return [float(np.float32(c)) for c in series.convert(kind=np.polynomial.Polynomial).coef]


COS = fitted(lambda y: np.cos(2 * np.pi * np.sqrt(y)), 5)
SIN = fitted(lambda y: np.sin(2 * np.pi * np.sqrt(y)) / np.sqrt(y), 5)


def horner(coefs, y):
    value = coefs[-1] * y + coefs[-2]
    for c in coefs[-3::-1]:
        value = value * y + c
    return value


def tn(a, b):
    return lax.dot_general(a, b, (((0,), (0,)), ((), ())), preferred_element_type=F32)


def nt(a, b):
    return lax.dot_general(a, b, (((1,), (1,)), ((), ())), preferred_element_type=F32)


def nn(a, b):
    return jnp.dot(a, b, preferred_element_type=F32)


def transposed(a):
    return jnp.transpose(a.astype(F32)).astype(a.dtype)


def kernel(
    feat_h, frac_h, kint_h, kern_h, dist_h, nbr_h, send_h, counts_h, cot_h, wmsg_h, wrad_h, wq_h, wo_h,
    gf_out, gmsg_out, rad_out, gwq_out, gwo_out,
    feat, frac, kint, kern, dist, nbr, send, counts, cot, wmsg, wrad, wq, wo,
    gf, gmsg_s, rad_s, gwq, gwo,
    table, sg_b, rc, xs, xs_b, rx, ag,
    fg, place_t, out_b, ghost, u_own, u_ghost,
    split_k, split_f, dz, env, lo_s, code_s, own_w, gmat, amat, ymat, gul, gug, radacc, gh_b, back, p_t, m_s,
    ar, ar1, ar2, fin, in_sem, out_sem, send_sem, recv_sem, rs_send, rs_recv, ag_send, ag_recv,
):
    pairs = [
        (kint_h, kint), (frac_h, frac), (counts_h, counts), (feat_h, feat), (cot_h, cot), (send_h, send),
        (dist_h, dist), (nbr_h, nbr), (wmsg_h, wmsg), (wrad_h, wrad), (kern_h, kern), (wq_h, wq), (wo_h, wo),
    ]
    loads = [pltpu.make_async_copy(src, dst, in_sem.at[i]) for i, (src, dst) in enumerate(pairs)]
    for c in loads:
        c.start()

    dom, sub = lax.axis_index("dom"), lax.axis_index("sub")
    x, zlo, y = dom // 8, (dom // 4) % 2, dom % 4
    zhi, core = sub // 2, sub % 2
    z = zhi * 2 + zlo
    yz = y * 4 + z
    chip = x * YZ + yz
    flat = dom * 4 + sub

    px = [(x + d) % 4 for d in range(4)]
    py = [(y + d) % 4 for d in range(4)]
    pz = [(z + d) % 4 for d in range(4)]
    far = [p * 8 for p in px]
    along = [(p % 2) * 4 for p in pz]
    pair_of = [(p // 2) * 2 for p in pz]
    both_cores = [core, 1 - core]

    def shifted(dx, dy, dz_, dc=0):
        where = (far[dx] + (along[dz_] + py[dy]), pair_of[dz_] + both_cores[dc])
        return px[dx] * YZ + (py[dy] * 4 + pz[dz_]), where

    def hops(turn):
        return sum(min(d, 4 - d) for d in turn)

    steps = (2, 1, 3, 0)
    turns = [(a, b, c) for a in range(4) for b in range(4) for c in range(4) if a or b or c]
    turns = sorted(turns, key=lambda t: (steps.index(t[0]), -hops(t)))
    places = [shifted(*t) for t in turns]
    plane = [(t, p) for t, p in zip(turns, places) if not t[0]]
    across = [(dx, dc) for dx in (2, 1, 3, 0) for dc in (1, 0) if dx or dc]
    across = [shifted(dx, 0, 0, dc)[1] for dx, dc in across]

    def group_of(dx):
        return [i for i, t in enumerate(turns) if t[0] == dx]

    other_core = (dom, zhi * 2 + 1 - core)
    upper, lower = (flat + 1) % 128, (flat + 127) % 128
    upper, lower = (upper // 4, upper % 4), (lower // 4, lower % 4)
    across = [(dx, dc) for dx in (2, 1, 3, 0) for dc in (1, 0) if dx or dc]
    across = [shifted(dx, 0, 0, dc)[1] for dx, dc in across]

    barrier = pltpu.get_barrier_semaphore()

    def greet(peer):
        pl.semaphore_signal(barrier, inc=1, device_id=peer, device_id_type=MESH)

    for _, peer in places:
        greet(peer)
    for peer in (upper, lower, other_core):
        greet(peer)
    for dx in range(1, X):
        greet(shifted(dx, 0, 0, 1)[1])
    greeted = CHIPS - 1 + 3 + X - 1

    sems = iter(range(48))

    def copy(src, dst, peer):
        at = next(sems)
        return pltpu.make_async_remote_copy(
            src_ref=src, dst_ref=dst, send_sem=send_sem.at[at], recv_sem=recv_sem.at[at],
            device_id=peer, device_id_type=MESH,
        )

    loads[0].wait()
    loads[1].wait()
    part = frac[...]
    blank = jnp.zeros((5, WIDTH), F32)
    pieces = []
    for _ in range(3):
        high = part.astype(BF).astype(F32)
        pieces += [high, blank]
        part = part - high
    split_f[...] = jnp.concatenate(pieces + [jnp.zeros((8, WIDTH), F32)], axis=0).astype(BF)
    k_rows = jnp.concatenate([kint[...].astype(F32), jnp.zeros((5, KCOUNT), F32)], axis=0)
    split_k[...] = jnp.concatenate([k_rows] * 3 + [jnp.zeros((8, KCOUNT), F32)], axis=0).astype(BF)

    def table_rows(step, _):
        base = pl.multiple_of(step * 256, 256)
        ks = split_k[:, pl.ds(base, 256)]
        for block in range(4):
            cols = slice(block * 128, block * 128 + 128)
            turns = tn(ks, split_f[:, cols])
            turns = turns - jnp.floor(turns + 0.5)
            square = turns * turns
            table[pl.ds(base, 256), cols] = horner(COS, square).astype(BF)
            table[pl.ds(KCOUNT + base, 256), cols] = (horner(SIN, square) * turns).astype(BF)
        return 0

    lax.fori_loop(0, KCOUNT // 256, table_rows, 0)

    for c in loads[2:5]:
        c.wait()
    live = lax.broadcasted_iota(jnp.int32, (WIDTH, CHANS), 0) < counts[0]
    fg[:, :CHANS] = jnp.where(live, feat[...].astype(F32), 0.0).astype(BF)
    fg[:, CHANS:] = jnp.where(live, cot[...].astype(F32), 0.0).astype(BF)
    theirs = pl.multiple_of((1 - core) * KCOUNT, KCOUNT)
    mine = pl.multiple_of(core * KCOUNT, KCOUNT)
    sg_b[...] = nn(table[pl.ds(theirs, KCOUNT), :], fg[...]).astype(BF)
    xs[...] = nn(table[pl.ds(mine, KCOUNT), :], fg[...])

    loads[5].wait()
    picks = jnp.concatenate([send[0:1, :], send[1:2, :]], axis=1)
    place_t[...] = jnp.where(
        lax.broadcasted_iota(jnp.int32, (WIDTH, 2 * GHOSTS), 0) == picks, 1.0, 0.0
    ).astype(BF)
    out_b[...] = tn(place_t[...], feat[...]).astype(BF)

    pl.semaphore_wait(barrier, greeted)

    halo = [
        copy(out_b.at[pl.ds(0, GHOSTS)], ghost.at[pl.ds(GHOSTS, GHOSTS)], lower),
        copy(out_b.at[pl.ds(GHOSTS, GHOSTS)], ghost.at[pl.ds(0, GHOSTS)], upper),
    ]
    quarters = [pl.ds(pl.multiple_of(px[dx] * QUART, QUART), QUART) for dx in range(4)]
    cores = [copy(sg_b.at[quarters[dx]], rc.at[quarters[dx]], other_core) for dx in steps]
    for c in cores[:2] + halo + cores[2:]:
        c.start()
    scatters = [
        pltpu.make_async_remote_copy(
            src_ref=xs_b.at[pl.ds(pl.multiple_of(to * PIECE, PIECE), PIECE)], dst_ref=rx.at[i],
            send_sem=rs_send.at[i], recv_sem=rs_recv.at[i], device_id=peer, device_id_type=MESH,
        )
        for i, (to, peer) in enumerate(places)
    ]
    for c in loads[6:]:
        c.wait()

    def spread_setup(pair):
        d_parts, p_parts = [], []
        for i in range(2):
            blk = 2 * pair + i
            w = min(max(blk * BLOCK - BLOCK // 2, 0), WIDTH - WINDOW)
            cols = slice(blk * BLOCK, (blk + 1) * BLOCK)
            n = nbr[:, cols]
            d_parts.append(dist[:, cols])
            place = jnp.where(n >= WIDTH, n - (WIDTH - WINDOW), n - w) + i * 2 * WINDOW
            p_parts.append(place.astype(F32))
        d2 = jnp.transpose(jnp.concatenate(d_parts, axis=0))
        place = jnp.concatenate(p_parts, axis=0)
        code = jnp.floor(place * (1.0 / 128.0))
        dz[pair] = d2 * (1.0 / 0.4)
        env[pair] = jnp.square(jnp.maximum(0.0, 1.0 - d2 * (1.0 / 6.0)))
        lo_s[pair] = place - code * 128.0
        code_s[pair] = jnp.transpose(code)

    def spread_blocks(first, last):
        many = 64

        def group(step, _):
            pair = step // 2
            base = pl.multiple_of(step % 2 * many, many)
            rows = pl.ds(base, many)
            dz_r, env_r, code_r = dz[pair, rows, :], env[pair, rows, :], code_s[pair, rows, :]
            lo_c = pltpu.roll(lo_s[pair], lax.rem(BLOCK - base, BLOCK), 1)
            b_ids = lax.broadcasted_iota(jnp.int32, (NB, 128), 0).astype(F32)
            lane = lax.broadcasted_iota(jnp.int32, (128, 128), 1).astype(F32).astype(BF)
            one, zero = jnp.ones((128, 128), BF), jnp.zeros((128, 128), BF)
            for s in range(many):
                gap = dz_r[s : s + 1, :] - b_ids
                basis = (jnp.exp(-(gap * gap)) * env_r[s : s + 1, :]).astype(BF)
                code = jnp.broadcast_to(code_r[s : s + 1, :], (NB, 128)).astype(BF)
                lhs = jnp.concatenate(
                    [jnp.where(code == h, basis, jnp.zeros_like(basis)) for h in range(8)], axis=0
                )
                low = jnp.broadcast_to(lo_c[:, s : s + 1], (128, 128)).astype(BF)
                out = nn(lhs, jnp.where(lane == low, one, zero)).astype(BF)
                for i in range(2):
                    at = pl.multiple_of((2 * pair + i) * BLOCK * NB + base * NB + s * NB, NB)
                    for h in range(4):
                        r = (i * 4 + h) * NB
                        gmat[pl.ds(at, NB), h * 128 : h * 128 + 128] = out[r : r + NB, :]
            return 0

        lax.fori_loop(first, last, group, 0)

    spread_setup(0)
    spread_setup(1)

    weights = kern[...] * (1.0 / math.sqrt(KCOUNT * TOTAL))
    weights = pltpu.roll(weights, lax.rem(KCOUNT - chip * PIECE, KCOUNT), 1)[:, :CHANS]
    own_w[...] = jnp.transpose(jnp.broadcast_to(weights, (CHANS, CHANS)))[:PIECE, :]

    spread_blocks(0, 1)

    for dx, c in zip(steps, cores):
        c.wait()
        val = xs[quarters[dx], :] + rc[quarters[dx], :].astype(F32)
        xs_b[quarters[dx], :] = val.astype(BF)
        if not dx:
            xs[quarters[dx], :] = val
        for i in group_of(dx):
            scatters[i].start()

    spread_blocks(1, 4)

    u_own[...] = nn(feat[...], wmsg[...]).astype(BF)
    gul[...] = jnp.zeros_like(gul)
    gug[...] = jnp.zeros_like(gug)
    radacc[...] = jnp.zeros_like(radacc)
    wr = wrad[...].astype(F32)

    def window_of(blk):
        return pl.ds(min(max(blk * BLOCK - BLOCK // 2, 0), WIDTH - WINDOW), WINDOW)

    def rows_of(blk):
        return pl.ds(blk * BLOCK * NB, BLOCK * NB)

    blocks = WIDTH // BLOCK
    for blk in range(blocks):
        amat[rows_of(blk), :] = nn(gmat[rows_of(blk), :WINDOW], u_own[window_of(blk), :])
    for c in halo:
        c.wait()
    u_ghost[...] = nn(ghost[...], wmsg[...]).astype(BF)

    def gathered(blk):
        amat[rows_of(blk), :] += nn(gmat[rows_of(blk), WINDOW:], u_ghost[...])

    def atoms(blk):
        piece = 32
        for step in range(BLOCK // piece):
            at = blk * BLOCK + step * piece
            rows = pl.ds(at * NB, piece * NB)
            summed = amat[rows, :].reshape(piece, NB, CHANS)
            pre = jnp.sum(summed * wr[None], axis=1)
            sig = 1.0 / (1.0 + jnp.exp(-pre))
            gpre = fg[pl.ds(at, piece), CHANS:].astype(F32) * sig * (1.0 + pre * (1.0 - sig))
            wide = gpre[:, None, :]
            radacc[...] += jnp.sum(wide * summed, axis=0)
            ymat[rows, :] = (wide * wr[None]).reshape(piece * NB, CHANS).astype(BF)

    def scattered(blk):
        collected = jnp.transpose(tn(ymat[rows_of(blk), :], gmat[rows_of(blk), :]))
        gul[window_of(blk), :] += collected[:WINDOW, :]
        gug[...] += collected[WINDOW:, :]

    gathered(0)
    for blk in range(blocks):
        if blk + 1 < blocks:
            gathered(blk + 1)
        atoms(blk)
        if blk:
            scattered(blk - 1)
    scattered(blocks - 1)

    gu_g = gug[...].astype(BF)
    gu_l = gul[...].astype(BF)
    gmsg = tn(feat[...], gu_l) + tn(ghost[...], gu_g)

    ar[:, 0:16, :] = gmsg.reshape(8, 16, CHANS)
    ar[:, 16:24, :] = jnp.zeros((8, 8, CHANS), F32)
    for j in range(8):
        ar[j, 16:18, :] = radacc[2 * j : 2 * j + 2, :]
    me = x * 2 + core
    ar_first = []
    for o, peer in enumerate(across):
        ar_first.append(copy(ar.at[lax.rem(peer[0], 32) // 8 * 2 + lax.rem(peer[1], 2)], ar1.at[o], peer))
    for c in ar_first:
        c.start()

    gh_b[...] = nt(gu_g, wmsg[...]).astype(BF)
    returns = [
        copy(gh_b.at[pl.ds(0, GHOSTS)], back.at[pl.ds(GHOSTS, GHOSTS)], lower),
        copy(gh_b.at[pl.ds(GHOSTS, GHOSTS)], back.at[pl.ds(0, GHOSTS)], upper),
    ]
    for c in returns:
        c.start()

    gul[...] = fg[:, CHANS:].astype(F32) + nt(gu_l, wmsg[...])

    for c in scatters:
        c.wait()
    own = xs[pl.ds(pl.multiple_of(chip * PIECE, PIECE), PIECE), :]
    def add_some(step, total):
        for j in range(9):
            total = total + rx[step * 9 + j].astype(F32)
        return total

    own = lax.fori_loop(0, (CHIPS - 1) // 9, add_some, own)
    at_piece = pl.ds(pl.multiple_of(mine + chip * PIECE, PIECE), PIECE)
    ag[at_piece, :CHANS] = own[:, :CHANS].astype(BF)
    ag[at_piece, CHANS:] = (own[:, CHANS:] * own_w[...]).astype(BF)
    gathers = [
        pltpu.make_async_remote_copy(
            src_ref=ag.at[at_piece], dst_ref=ag.at[at_piece],
            send_sem=ag_send.at[i], recv_sem=ag_recv.at[i], device_id=peer, device_id_type=MESH,
        )
        for i, (_, peer) in enumerate(places)
    ]
    for c in gathers:
        c.start()


    for c in ar_first:
        c.wait()
    val = ar[me]
    for o in range(7):
        val = val + ar1[o]
    ar2[yz] = jnp.concatenate([val, jnp.zeros((8, CHANS), F32)], axis=0).astype(BF)
    ar_yz = [copy(ar2.at[yz], ar2.at[yz], peer) for _, (_, peer) in plane]
    for c in ar_yz:
        c.start()

    for c in ar_yz:
        c.wait()
    val = ar2[0].astype(F32)
    for j in range(1, YZ):
        val = val + ar2[j].astype(F32)
    fin[me] = val.astype(BF)
    ar_fin = [copy(fin.at[me], fin.at[me], peer) for peer in across]
    for c in ar_fin:
        c.start()
    passed = []
    for dx in steps:
        for i in group_of(dx):
            gathers[i].wait()
        rows = pl.ds(pl.multiple_of(mine + px[(4 - dx) % 4] * QUART, QUART), QUART)
        passed.append(copy(ag.at[rows], ag.at[rows], other_core))
        passed[-1].start()

    def half_of(start, which):
        rows = pl.ds(start, KCOUNT)
        weighted = ag[rows, CHANS:]
        m_s[which] = tn(weighted, ag[rows, :CHANS])
        return tn(weighted, table[rows, :])

    p_t[...] = half_of(mine, core)
    for c in passed:
        c.wait()
    p_b = (p_t[...] + half_of(theirs, 1 - core)).astype(BF)
    gq_t = nn(wo[...], p_b).astype(BF)
    ghq = jnp.transpose(nn(wq[...], gq_t))
    base_grad = gul[...] + jnp.where(live, ghq, 0.0)
    for c in returns:
        c.wait()
    gf[...] = base_grad + nn(place_t[...], back[...])
    outs = [
        pltpu.make_async_copy(src, dst, out_sem.at[i])
        for i, (src, dst) in enumerate(
            [(gf, gf_out), (gwq, gwq_out), (gwo, gwo_out), (gmsg_s, gmsg_out), (rad_s, rad_out)]
        )
    ]
    outs[0].start()

    rscale = 1.0 / math.sqrt(TOTAL)
    m_full = jnp.transpose(m_s[0] + m_s[1])
    m_hi = m_full.astype(BF)
    m_lo = (m_full - m_hi.astype(F32)).astype(BF)
    gwq[...] = (nt(m_hi, wo[...]) + nt(m_lo, wo[...])) * rscale
    wq_t = transposed(wq[...])
    gwo[...] = (nn(wq_t, m_hi) + nn(wq_t, m_lo)) * rscale
    outs[1].start()
    outs[2].start()

    for c in ar_fin:
        c.wait()
    gmsg_s[...] = fin[:, 0:16, :].astype(F32).reshape(CHANS, CHANS) * rscale
    outs[3].start()
    for j in range(8):
        rad_s[2 * j : 2 * j + 2, :] = fin[j, 16:32, :].astype(F32)[0:2, :] * (rscale / math.sqrt(SLOTS))
    outs[4].start()
    for c in outs:
        c.wait()


def finish(*refs):
    ins, outs, held, sem = refs[:5], refs[5:10], refs[10:15], refs[15]
    reads = [pltpu.make_async_copy(ins[i], held[i], sem.at[i]) for i in range(5)]
    writes = [pltpu.make_async_copy(held[i], outs[i], sem.at[5 + i]) for i in range(5)]
    for r in reads:
        r.start()
    for r, w in zip(reads, writes):
        r.wait()
        w.start()
    for w in writes:
        w.wait()


def on_device(features, frac, k_int, kern, dist, nbr, send_index, counts, cot, w_msg, w_rad, w_q, w_o):
    hbm = pl.BlockSpec(memory_space=pltpu.HBM)

    def buf(*shape, dtype=BF):
        return pltpu.VMEM(shape, dtype)

    def result(*shape):
        return jax.ShapeDtypeStruct(shape, F32)

    shapes = (result(WIDTH, CHANS), result(CHANS, CHANS), result(NB, CHANS), result(CHANS, CHANS), result(CHANS, CHANS))
    sums = pl.pallas_call(
        kernel,
        out_shape=shapes,
        in_specs=[hbm] * 13,
        out_specs=(hbm,) * 5,
        scratch_shapes=[
            buf(WIDTH, CHANS),
            buf(3, WIDTH, dtype=F32),
            buf(3, KCOUNT, dtype=jnp.int32),
            buf(1, KCOUNT, dtype=F32),
            buf(SLOTS, WIDTH, dtype=F32),
            buf(SLOTS, WIDTH, dtype=jnp.int32),
            buf(2, GHOSTS, dtype=jnp.int32),
            pltpu.SMEM((1,), jnp.int32),
            buf(WIDTH, CHANS),
            buf(CHANS, CHANS),
            buf(NB, CHANS),
            buf(CHANS, CHANS),
            buf(CHANS, CHANS),
            buf(WIDTH, CHANS, dtype=F32),
            buf(CHANS, CHANS, dtype=F32),
            buf(NB, CHANS, dtype=F32),
            buf(CHANS, CHANS, dtype=F32),
            buf(CHANS, CHANS, dtype=F32),
            buf(2 * KCOUNT, WIDTH),
            buf(KCOUNT, BOTH),
            buf(KCOUNT, BOTH),
            buf(KCOUNT, BOTH, dtype=F32),
            buf(KCOUNT, BOTH),
            buf(CHIPS - 1, PIECE, BOTH),
            buf(2 * KCOUNT, BOTH),
            buf(WIDTH, BOTH),
            buf(WIDTH, 2 * GHOSTS),
            buf(2 * GHOSTS, CHANS),
            buf(2 * GHOSTS, CHANS),
            buf(WIDTH, CHANS),
            buf(2 * GHOSTS, CHANS),
            buf(32, KCOUNT),
            buf(32, WIDTH),
            buf(2, BLOCK, 128, dtype=F32),
            buf(2, BLOCK, 128, dtype=F32),
            buf(2, BLOCK, 128, dtype=F32),
            buf(2, BLOCK, 128, dtype=F32),
            buf(PIECE, CHANS, dtype=F32),
            buf(WIDTH * NB, 2 * WINDOW),
            buf(WIDTH * NB, CHANS, dtype=F32),
            buf(WIDTH * NB, CHANS),
            buf(WIDTH, CHANS, dtype=F32),
            buf(2 * GHOSTS, CHANS, dtype=F32),
            buf(NB, CHANS, dtype=F32),
            buf(2 * GHOSTS, CHANS),
            buf(2 * GHOSTS, CHANS),
            buf(CHANS, WIDTH, dtype=F32),
            buf(2, CHANS, CHANS, dtype=F32),
            buf(8, ROWS_AR, CHANS, dtype=F32),
            buf(7, ROWS_AR, CHANS, dtype=F32),
            buf(YZ, 32, CHANS),
            buf(8, 32, CHANS),
            pltpu.SemaphoreType.DMA((13,)),
            pltpu.SemaphoreType.DMA((5,)),
            pltpu.SemaphoreType.DMA((48,)),
            pltpu.SemaphoreType.DMA((48,)),
            pltpu.SemaphoreType.DMA((CHIPS - 1,)),
            pltpu.SemaphoreType.DMA((CHIPS - 1,)),
            pltpu.SemaphoreType.DMA((CHIPS - 1,)),
            pltpu.SemaphoreType.DMA((CHIPS - 1,)),
        ],
        compiler_params=pltpu.CompilerParams(
            collective_id=0, has_side_effects=True, vmem_limit_bytes=VMEM_BYTES
        ),
        name="ewald_backward",
    )(
        features, frac, k_int, kern.reshape(1, KCOUNT), dist.T, nbr.T,
        send_index.reshape(2, GHOSTS), counts, cot, w_msg, w_rad, w_q, w_o,
    )
    return pl.pallas_call(
        finish,
        out_shape=shapes,
        in_specs=[hbm] * 5,
        out_specs=(hbm,) * 5,
        scratch_shapes=[buf(*t.shape, dtype=F32) for t in shapes] + [pltpu.SemaphoreType.DMA((10,))],
        compiler_params=pltpu.CompilerParams(vmem_limit_bytes=VMEM_BYTES),
        name="finish",
    )(*sums)


def solution(mesh):
    rows = P(("dom", "sub"), None)
    placed = (
        rows, P(None, ("dom", "sub")), P(), P(), rows, rows,
        P(("dom", "sub"), None, None), P(("dom", "sub")), rows, P(), P(), P(), P(),
    )
    return jax.shard_map(
        on_device,
        mesh=mesh,
        in_specs=placed,
        out_specs=(rows, P(), P(), P(), P()),
        check_vma=False,
    )
```
